32 devices in a mesh: rep: 2 (over y), dp: 8 (over z, x), tensor: 2 (over core).
Axes of the slice: x: 2, y: 2, z: 4, core: 2. Of those that a mesh axis runs over, the one named last changes fastest.
Arguments:
- queries: bfloat16 [32, 256, 2048], P(('rep', 'dp'), None, 'tensor'), parts along dimension 0, may hold values from -18 to 18
- key_rows: bfloat16 [32, 256, 2048], P(('rep', 'dp'), None, 'tensor'), parts along dimension 0, may hold values from -4 to 4
- values: bfloat16 [32, 256, 2048], P(('rep', 'dp'), None, 'tensor'), parts along dimension 0, may hold values from -5 to 5
- position_bias: float32 [32, 32], P(None, 'tensor'), may hold values from -3 to 3
- out_weight: bfloat16 [2048, 2048], P('tensor', 'dp'), may hold values from -1 to 1
- counts: int32 [16], P(('rep', 'dp')), parts along dimension 0, may hold values from 0 to 2, as said below
- donors: int32 [8], P('rep'), parts along dimension 0, may hold values from 0 to 7, as said below
Outputs:
- encoded: bfloat16 [32, 256, 2048], P(('rep', 'dp'), None, 'tensor'), parts along dimension 0
The draws below stay inside these ranges and needn't reach their ends.
There are 2 independent parts, one for each index of `rep`. The reference program is written for one: setup_inputs(seed, part) draws one part's arguments, and reference() takes and returns one part's arrays. A program takes and returns all parts, laid end to end along the dimension named above; an argument that names none is the same for every part. Nothing has to cross between parts.
Inputs may be any that keep to these rules, and one draw needn't show every extreme that they name: `counts`: exactly 4 data groups hold 2 passages, the others 0 or 1. `donors`: the data groups whose count is 2, ascending.
All inputs are finite; a program needn't handle non-finite values.
Results may differ from the reference program's by a relative error of at most 0.013.
Values may be sent and summed in bfloat16 or wider, within the bound.
No kernel may reach another device: no remote copies, remote signals or barrier semaphores. Data moves between devices by JAX's collectives and lax.ppermute only.
A program may use at most 64 MiB of HBM per device.

```python
import jax
import jax.numpy as jnp
from jax import lax

D = 2048
HEADS = 32
HEAD_DIM = 64
P_SIZE = 256
SLOTS = 2
BUCKETS = 32
INNER = 2048
PASSAGES = 16
N_DP = 8


def shared_base(key):
    base = jax.random.normal(key, (PASSAGES, P_SIZE, INNER), jnp.float32)
    return jnp.clip(base, -4.0, 4.0)


def pick_donors(key):
    order = jax.random.permutation(key, N_DP)
    return jnp.sort(order[:N_DP // 2])


def draw_key_rows(key, part):
    base = shared_base(key)
    return base.astype(jnp.bfloat16)


def draw_queries(key, part):
    key = jax.random.fold_in(key, 12)
    result = 0.125 * jnp.clip(jax.random.normal(key, (PASSAGES, P_SIZE, INNER), jnp.float32), -4.0, 4.0)
    return result.astype(jnp.bfloat16)


def draw_donors(key, part):
    chosen = pick_donors(key)
    return chosen.astype(jnp.int32)


def draw_counts(key, part):
    chosen = pick_donors(key)
    key = jax.random.fold_in(key, 22)
    lighter = jax.random.randint(key, (N_DP,), 0, 2)
    flagged = jnp.zeros((N_DP,), jnp.int32).at[chosen].set(1)
    return jnp.where(flagged == 1, 2, lighter).astype(jnp.int32)


def steps_of(rng, shape, shards, least, high):
    def one(dim, shards_of):
        draws = jax.random.uniform(jax.random.fold_in(jax.random.fold_in(rng, 6), dim), (shards_of,), jnp.float32, least / len(shards), high / len(shards))
        return jnp.repeat(jnp.exp(draws), shape[dim] // shards_of).reshape((-1,) + (1,) * (len(shape) - dim - 1))

    gain = one(*shards[0])
    for cut in shards[1:]:
        gain = gain * one(*cut)
    return gain


def normal_values(key, extent, scale, most, shards=(), kind=jnp.bfloat16):
    level = steps_of(key, extent, shards, -0.22, 0.18) if shards else 1.0
    values = jax.random.normal(key, extent, jnp.float32) * scale * level
    return jnp.minimum(jnp.maximum(values, -most), most).astype(kind)


def setup_inputs(seed: int = 0, part: int = 0) -> dict:
    key_of = jax.random.split(jax.random.key(seed), 8)
    own_keys = jax.random.split(jax.random.fold_in(key_of[7], part), 8)
    queries = draw_queries(jax.random.fold_in(jax.random.fold_in(key_of[7], part), 71), part)
    key_rows = draw_key_rows(jax.random.fold_in(jax.random.fold_in(key_of[7], part), 71), part)
    values = normal_values(own_keys[2], (PASSAGES, P_SIZE, INNER), 1.0, 5.0, ((0, 8), (2, 2)))
    position_bias = normal_values(key_of[3], (BUCKETS, HEADS), 0.5, 3.0, ((1, 2),), jnp.float32)
    out_weight = normal_values(key_of[4], (INNER, D), (INNER // 64) ** -0.5, 1.0, ((0, 2), (1, 8)))
    counts = draw_counts(jax.random.fold_in(jax.random.fold_in(key_of[7], part), 71), part)
    donors = draw_donors(jax.random.fold_in(jax.random.fold_in(key_of[7], part), 71), part)
    return {"queries": queries, "key_rows": key_rows, "values": values, "position_bias": position_bias, "out_weight": out_weight, "counts": counts, "donors": donors}


def position_buckets(length):
    position = jnp.arange(length, dtype=jnp.int32)
    relative = position[None, :] - position[:, None]
    distance = jnp.abs(relative)
    far_bucket = 8 + sum((distance >= threshold).astype(jnp.int32) for threshold in (12, 16, 23, 32, 46, 64, 91))
    near_bucket = jnp.where(distance < 8, distance, far_bucket)
    return near_bucket + 16 * (relative > 0).astype(jnp.int32)


def reference(queries, key_rows, values, position_bias, out_weight, counts, donors):
    buckets = position_buckets(P_SIZE)
    one_hot = (buckets[:, :, None] == jnp.arange(BUCKETS, dtype=jnp.int32)[None, None, :]).astype(jnp.float32)
    position_terms = jnp.einsum("ijb,bh->hij", one_hot, position_bias, precision=lax.Precision.HIGHEST)
    half_inner = INNER // 2

    def encode(index):
        query = queries[index].astype(jnp.float32).reshape(P_SIZE, HEADS, HEAD_DIM)
        keyed = key_rows[index].astype(jnp.float32).reshape(P_SIZE, HEADS, HEAD_DIM)
        valued = values[index].astype(jnp.float32).reshape(P_SIZE, HEADS, HEAD_DIM)
        scores = jnp.einsum("ihd,jhd->hij", query, keyed) + position_terms
        highest = jnp.max(scores, axis=-1, keepdims=True)
        expd = jnp.exp(scores - highest)
        attention = (expd / jnp.sum(expd, axis=-1, keepdims=True)).astype(jnp.bfloat16)
        context = jnp.einsum("hij,jhd->ihd", attention.astype(jnp.float32), valued)
        context = context.astype(jnp.bfloat16).reshape(P_SIZE, INNER)
        lower = jnp.dot(context[:, :half_inner], out_weight[:half_inner], preferred_element_type=jnp.float32).astype(jnp.bfloat16)
        upper = jnp.dot(context[:, half_inner:], out_weight[half_inner:], preferred_element_type=jnp.float32).astype(jnp.bfloat16)
        return (lower.astype(jnp.float32) + upper.astype(jnp.float32)).astype(jnp.bfloat16)

    encoded = lax.map(encode, jnp.arange(PASSAGES, dtype=jnp.int32))
    slot_index = jnp.arange(PASSAGES, dtype=jnp.int32) % SLOTS
    group_index = jnp.arange(PASSAGES, dtype=jnp.int32) // SLOTS
    first_live = (slot_index == 0) & (counts[group_index] >= 1)
    second_live = (slot_index == 1) & jnp.any(group_index[:, None] == donors[None, :], axis=1)
    live_mask = (first_live | second_live).astype(jnp.bfloat16)
    return encoded * live_mask[:, None, None]
```

```python
import functools

import jax
import jax.numpy as jnp
from jax import lax
from jax.experimental import pallas as pl
from jax.experimental.pallas import tpu as pltpu
from jax.sharding import PartitionSpec as P

HEAD_DIM = 64
PAIR = 2 * HEAD_DIM
CHUNK = 256
THRESHOLDS = (12, 16, 23, 32, 46, 64, 91)
AXES = ("rep", "dp", "tensor")


def bias_rows(position_bias, tokens):
    bucket_count = position_bias.shape[0]
    shape = (bucket_count, 2 * tokens)
    relative = lax.broadcasted_iota(jnp.int32, shape, 1) - (tokens - 1)
    distance = jnp.abs(relative)
    far = jnp.full(shape, 8, jnp.int32)
    for threshold in THRESHOLDS:
        far = far + jnp.where(distance >= threshold, 1, 0)
    bucket = jnp.where(distance < 8, distance, far) + jnp.where(relative > 0, 16, 0)
    one_hot = jnp.where(bucket == lax.broadcasted_iota(jnp.int32, shape, 0), 1.0, 0.0)
    return lax.dot_general(
        position_bias,
        one_hot,
        (((0,), (0,)), ((), ())),
        precision=lax.Precision.HIGHEST,
        preferred_element_type=jnp.float32,
    )


def attention_kernel(first_head, bias_ref, query_ref, key_ref, value_ref, out_ref):
    slots, tokens, width = query_ref.shape
    rows = bias_rows(bias_ref[...], tokens)
    lower = lax.broadcasted_iota(jnp.int32, (tokens, PAIR), 1) < HEAD_DIM
    for pair in range(width // PAIR):
        columns = slice(pair * PAIR, (pair + 1) * PAIR)
        terms = []
        for head in range(2):
            at = first_head + 2 * pair + head
            spread = jnp.broadcast_to(rows[at : at + 1], (tokens, 2 * tokens))
            rolled = pltpu.roll(spread, tokens + 1, 1, stride=1, stride_axis=0)
            terms.append(rolled[:, :tokens])
        for slot in range(slots):
            query = query_ref[slot, :, columns]
            key = key_ref[slot, :, columns]
            value = value_ref[slot, :, columns]
            sums = []
            for head in range(2):
                own = lower if head == 0 else jnp.logical_not(lower)
                scores = lax.dot_general(
                    query,
                    jnp.where(own, key, 0),
                    (((1,), (1,)), ((), ())),
                    preferred_element_type=jnp.float32,
                )
                scores = scores + terms[head]
                highest = jnp.max(scores, axis=-1, keepdims=True)
                expd = jnp.exp(scores - highest).astype(jnp.bfloat16)
                sums.append(
                    jnp.dot(expd, jnp.where(own, value, 1), preferred_element_type=jnp.float32)
                )
            weighted = jnp.where(lower, sums[0], sums[1])
            total = pltpu.roll(jnp.where(lower, sums[1], sums[0]), HEAD_DIM, 1)
            out_ref[slot * tokens : (slot + 1) * tokens, columns] = (weighted / total).astype(
                jnp.bfloat16
            )


def attend(queries, key_rows, values, position_bias, chunk):
    slots, tokens, _ = queries.shape
    block = pl.BlockSpec((slots, tokens, CHUNK), lambda i: (0, 0, chunk))
    heads = CHUNK // HEAD_DIM
    scores = slots * heads * tokens * tokens
    return pl.pallas_call(
        functools.partial(attention_kernel, chunk * heads),
        out_shape=jax.ShapeDtypeStruct((slots * tokens, CHUNK), jnp.bfloat16),
        grid=(1,),
        in_specs=[pl.BlockSpec(position_bias.shape, lambda i: (0, 0)), block, block, block],
        out_specs=pl.BlockSpec((slots * tokens, CHUNK), lambda i: (0, 0)),
        compiler_params=pltpu.CompilerParams(vmem_limit_bytes=24 << 20),
        cost_estimate=pl.CostEstimate(
            flops=4 * scores * HEAD_DIM,
            bytes_accessed=8 * slots * tokens * CHUNK,
            transcendentals=scores,
        ),
    )(position_bias, queries, key_rows, values)


def device_index(rep, dp, tensor, dp_size):
    return (rep * dp_size + dp) * 2 + tensor


def ring_order(dp_size):
    half = dp_size // 2
    return [2 * i for i in range(half)] + [2 * i + 1 for i in reversed(range(half))]


def ring_pairs(reps, dp_size, way):
    order = ring_order(dp_size)
    pairs = []
    for rep in range(reps):
        step = way if rep == 0 else -way
        for place in range(dp_size):
            to = order[(place + step) % dp_size]
            for tensor in range(2):
                pairs.append(
                    (
                        device_index(rep, order[place], tensor, dp_size),
                        device_index(rep, to, tensor, dp_size),
                    )
                )
    return pairs


def block_of(distance):
    dp = lax.axis_index("dp")
    place = jnp.where(dp % 2 == 0, dp // 2, 7 - dp // 2)
    way = jnp.where(lax.axis_index("rep") == 0, 1, -1)
    place = (place - way * distance + 16) % 8
    return jnp.where(place < 4, 2 * place, 2 * (7 - place) + 1)


def project_kernel(plan, n_weights, *refs):
    context = refs[:4]
    weights = refs[4 : 4 + n_weights]
    kept_ref, sent_ref, product, sem = refs[-4:]
    tensor = lax.axis_index("tensor")

    def copies(slot, block):
        column = pl.multiple_of((block % 4) * CHUNK, CHUNK)
        source = product.at[slot]
        return (
            pltpu.make_async_copy(source, kept_ref.at[:, pl.ds(column, CHUNK)], sem.at[slot]),
            pltpu.make_async_copy(source, sent_ref.at[:, pl.ds(column, CHUNK)], sem.at[slot]),
        )

    for slot, (distance, pieces) in enumerate(plan):
        total = None
        for weight, row, column, rows in pieces:
            part = jnp.dot(
                context[column // CHUNK][:, column % CHUNK : column % CHUNK + rows],
                weights[weight][row : row + rows],
                preferred_element_type=jnp.float32,
            )
            total = part if total is None else total + part
        product[slot] = total.astype(jnp.bfloat16)
        block = block_of(distance)
        kept, sent = copies(slot, block)

        @pl.when(block // 4 == tensor)
        def _():
            kept.start()

        @pl.when(block // 4 != tensor)
        def _():
            sent.start()

    for slot, (distance, _) in enumerate(plan):
        copies(slot, jnp.int32(0))[0].wait()


def project(context, weights, plan, held):
    rows = context[0].shape[0]
    wide = jax.ShapeDtypeStruct((rows, 4 * CHUNK), jnp.bfloat16)
    vmem = pl.BlockSpec(memory_space=pltpu.VMEM)
    away = pl.BlockSpec(memory_space=pl.ANY)
    n_in = 4 + len(weights)
    return pl.pallas_call(
        functools.partial(project_kernel, plan, len(weights)),
        out_shape=[wide, wide],
        in_specs=[vmem] * n_in + [away] * len(held),
        out_specs=[away, away],
        scratch_shapes=[
            pltpu.VMEM((len(plan), rows, CHUNK), jnp.bfloat16),
            pltpu.SemaphoreType.DMA((len(plan),)),
        ],
        input_output_aliases={n_in: 0, n_in + 1: 1} if held else {},
        compiler_params=pltpu.CompilerParams(vmem_limit_bytes=24 << 20),
        cost_estimate=pl.CostEstimate(
            flops=len(plan) * 2 * rows * 4 * CHUNK * CHUNK,
            bytes_accessed=len(plan) * 2 * (rows * CHUNK + 4 * CHUNK * CHUNK),
            transcendentals=0,
        ),
    )(*context, *weights, *held)


def finish_kernel(counts_ref, donors_ref, kept_ref, other_ref, out_ref):
    slots = out_ref.shape[0]
    tokens = out_ref.shape[1]
    my_group = lax.axis_index("dp")
    second = donors_ref[0] == my_group
    for at in range(1, donors_ref.shape[0]):
        second = jnp.logical_or(second, donors_ref[at] == my_group)
    live = [counts_ref[0] >= 1, second]
    for slot in range(slots):
        rows = slice(slot * tokens, (slot + 1) * tokens)
        both = kept_ref[rows].astype(jnp.float32) + other_ref[rows].astype(jnp.float32)
        both = both * jnp.where(live[slot], 1.0, 0.0)
        out_ref[slot] = both.astype(jnp.bfloat16)


def finish(kept, other, counts, donors, slots):
    rows, columns = kept.shape
    width = CHUNK
    tokens = rows // slots
    smem = pl.BlockSpec(memory_space=pltpu.SMEM)
    block = pl.BlockSpec((rows, width), lambda i: (0, i))
    return pl.pallas_call(
        finish_kernel,
        out_shape=jax.ShapeDtypeStruct((slots, tokens, columns), jnp.bfloat16),
        grid=(columns // width,),
        in_specs=[smem, smem, block, block],
        out_specs=pl.BlockSpec((slots, tokens, width), lambda i: (0, 0, i)),
    )(counts, donors, kept, other)


def with_ring(queries, key_rows, values, position_bias, out_weight, counts, donors, reps, dp_size):
    slots = queries.shape[0]
    ahead = ring_pairs(reps, dp_size, 1)
    back = ring_pairs(reps, dp_size, -1)
    across = [
        (device_index(r, d, t, dp_size), device_index(1 - r, d, t, dp_size))
        for r in range(2)
        for d in range(dp_size)
        for t in range(2)
    ]
    cores = [
        (device_index(r, d, t, dp_size), device_index(r, d, 1 - t, dp_size))
        for r in range(2)
        for d in range(dp_size)
        for t in range(2)
    ]
    send = lambda value, pairs: lax.ppermute(value, AXES, pairs)
    depth = out_weight.shape[0]
    cut = depth // 4

    def attention(chunk, held):
        return attend(queries, key_rows, values, held, chunk)

    upper, lower = out_weight[: depth - cut], out_weight[cut:]
    p1, q1 = send(upper, ahead), send(lower, back)
    c0 = attention(0, position_bias)
    c1 = attention(1, position_bias)
    p1, q1, c0, c1, bias = lax.optimization_barrier((p1, q1, c0, c1, position_bias))

    edge = lambda p, q: jnp.concatenate([p[:cut], q[-cut:]], axis=0)
    p2, q2, y1 = send(p1, ahead), send(q1, back), send(edge(p1, q1), across)
    c2 = attention(2, bias)
    c3 = attention(3, bias)
    p2, q2, y1, c2, c3 = lax.optimization_barrier((p2, q2, y1, c2, c3))
    context = (c0, c1, c2, c3)

    def block_pieces(p, y):
        head = [(p, CHUNK * i, CHUNK * i, CHUNK) for i in range(3)]
        return head + [(y, CHUNK, 3 * CHUNK, CHUNK)]

    def block_pieces_back(q, y):
        tail = [(q, CHUNK * i, CHUNK * (i + 1), CHUNK) for i in range(3)]
        return [(y, 0, 0, CHUNK)] + tail

    p3, q3, y2 = send(p2, ahead), send(q2, back), send(edge(p2, q2), across)
    own = [(0, CHUNK * i, CHUNK * i, CHUNK) for i in range(4)]
    held = project(
        context,
        (out_weight, p1, q1, y1),
        [(0, own), (1, block_pieces(1, 3)), (-1, block_pieces_back(2, 3))],
        (),
    )
    p3, q3, y2, held = lax.optimization_barrier((p3, q3, y2, held))

    half = depth // 2
    p4, q4 = send(p3[:half], ahead), send(q3[-half:], back)
    y3 = send(edge(p3, q3), across)
    held = project(
        context,
        (p2, q2, y2),
        [(2, block_pieces(0, 2)), (-2, block_pieces_back(1, 2))],
        held,
    )
    p4, q4, y3, held = lax.optimization_barrier((p4, q4, y3, held))
    opposite = [(3, 0, 0, CHUNK), (3, CHUNK, CHUNK, CHUNK)]
    opposite += [(4, 0, 2 * CHUNK, CHUNK), (4, CHUNK, 3 * CHUNK, CHUNK)]
    kept, sent = project(
        context,
        (p3, q3, y3, p4, q4),
        [(3, block_pieces(0, 2)), (-3, block_pieces_back(1, 2)), (4, opposite)],
        held,
    )
    return finish(kept, send(sent, cores), counts, donors, slots)


def with_gather(queries, key_rows, values, position_bias, out_weight, counts, donors):
    slots, tokens, features = queries.shape
    whole = lax.all_gather(out_weight, "dp", axis=1, tiled=True)
    context = jnp.concatenate(
        [attend(queries, key_rows, values, position_bias, i) for i in range(features // CHUNK)],
        axis=1,
    )
    product = jnp.dot(context, whole, preferred_element_type=jnp.float32).astype(jnp.bfloat16)
    merged = lax.psum_scatter(product, "tensor", scatter_dimension=1, tiled=True)
    first_live = counts[0] >= 1
    second_live = jnp.any(donors == lax.axis_index("dp"))
    live = jnp.stack([first_live, second_live]).astype(jnp.bfloat16)
    return merged.reshape(slots, tokens, merged.shape[1]) * live[:, None, None]


def solution(mesh):
    in_specs = (
        P(("rep", "dp"), None, "tensor"),
        P(("rep", "dp"), None, "tensor"),
        P(("rep", "dp"), None, "tensor"),
        P(None, "tensor"),
        P("tensor", "dp"),
        P(("rep", "dp")),
        P("rep"),
    )
    out_specs = P(("rep", "dp"), None, "tensor")
    reps, dp_size = mesh.shape["rep"], mesh.shape["dp"]
    if reps == 2 and dp_size == 8 and mesh.shape["tensor"] == 2:
        on_device = functools.partial(with_ring, reps=reps, dp_size=dp_size)
    else:
        on_device = with_gather
    return jax.shard_map(
        on_device, mesh=mesh, in_specs=in_specs, out_specs=out_specs, check_vma=False
    )
```

```python
import functools

import jax
import jax.numpy as jnp
from jax import lax
from jax.experimental import pallas as pl
from jax.experimental.pallas import tpu as pltpu
from jax.sharding import PartitionSpec as P

HEAD_DIM = 64
PAIR = 2 * HEAD_DIM
CHUNK = 256
THRESHOLDS = (12, 16, 23, 32, 46, 64, 91)
AXES = ("rep", "dp", "tensor")


def bias_rows(position_bias, tokens):
    bucket_count = position_bias.shape[1]
    shape = (bucket_count, 2 * tokens)
    relative = lax.broadcasted_iota(jnp.int32, shape, 1) - (tokens - 1)
    distance = jnp.abs(relative)
    far = jnp.full(shape, 8, jnp.int32)
    for threshold in THRESHOLDS:
        far = far + jnp.where(distance >= threshold, 1, 0)
    bucket = jnp.where(distance < 8, distance, far) + jnp.where(relative > 0, 16, 0)
    one_hot = jnp.where(bucket == lax.broadcasted_iota(jnp.int32, shape, 0), 1.0, 0.0)
    return lax.dot_general(
        position_bias,
        one_hot,
        (((1,), (0,)), ((), ())),
        precision=lax.Precision.HIGHEST,
        preferred_element_type=jnp.float32,
    )


def attention_kernel(first, bias_ref, *refs):
    sources, (out_ref, held, sem) = refs[:3], refs[-3:]
    count, _, slots, tokens, width = held.shape
    copies = [
        [
            pltpu.make_async_copy(
                source.at[:, :, (first + chunk) * width : (first + chunk + 1) * width],
                held.at[chunk, at],
                sem.at[chunk, at],
            )
            for at, source in enumerate(sources)
        ]
        for chunk in range(count)
    ]
    for chunk in copies:
        for copy in chunk:
            copy.start()
    rows = bias_rows(bias_ref[...], tokens)
    lower = lax.broadcasted_iota(jnp.int32, (tokens, PAIR), 1) < HEAD_DIM
    for chunk in range(count):
        for copy in copies[chunk]:
            copy.wait()
        for pair in range(width // PAIR):
            columns = slice(pair * PAIR, (pair + 1) * PAIR)
            head = (first + chunk) * (width // HEAD_DIM) + 2 * pair
            terms = [toeplitz(rows[head + i : head + i + 1], tokens) for i in range(2)]
            for slot in range(slots):
                query, key, value = (held[chunk, at, slot, :, columns] for at in range(3))
                sums = []
                for i in range(2):
                    own = lower if i == 0 else jnp.logical_not(lower)
                    scores = lax.dot_general(
                        query,
                        jnp.where(own, key, 0),
                        (((1,), (1,)), ((), ())),
                        preferred_element_type=jnp.float32,
                    )
                    scores = scores + terms[i]
                    highest = jnp.max(scores, axis=-1, keepdims=True)
                    expd = jnp.exp(scores - highest).astype(jnp.bfloat16)
                    sums.append(
                        jnp.dot(expd, jnp.where(own, value, 1), preferred_element_type=jnp.float32)
                    )
                weighted = jnp.where(lower, sums[0], sums[1])
                total = pltpu.roll(jnp.where(lower, sums[1], sums[0]), HEAD_DIM, 1)
                at = slice(chunk * width + pair * PAIR, chunk * width + (pair + 1) * PAIR)
                out_ref[slot * tokens : (slot + 1) * tokens, at] = (weighted / total).astype(
                    jnp.bfloat16
                )


def toeplitz(row, tokens):
    spread = jnp.broadcast_to(row, (8, 2 * tokens))
    base = pltpu.roll(spread, tokens + 1, 1, stride=1, stride_axis=0)
    rolled = [base if i == 0 else pltpu.roll(base, 8 * i, 1) for i in range(16)]
    groups = []
    for group in range(tokens // 8):
        turned, whole = rolled[group % 16], group // 16 * 128
        if whole:
            turned = jnp.concatenate([turned[:, -whole:], turned[:, : tokens - whole]], axis=1)
        groups.append(turned[:, :tokens])
    return jnp.concatenate(groups, axis=0)


def attend(queries, key_rows, values, position_bias, first, count, after=()):
    slots, tokens, _ = queries.shape
    vmem = pl.BlockSpec(memory_space=pltpu.VMEM)
    away = pl.BlockSpec(memory_space=pltpu.HBM)
    scores = slots * (CHUNK // HEAD_DIM) * tokens * tokens * count
    return pl.pallas_call(
        functools.partial(attention_kernel, first),
        out_shape=jax.ShapeDtypeStruct((slots * tokens, CHUNK * count), jnp.bfloat16),
        in_specs=[vmem] + [away] * 3 + [pl.BlockSpec(memory_space=pl.ANY)] * len(after),
        out_specs=vmem,
        scratch_shapes=[
            pltpu.VMEM((count, 3, slots, tokens, CHUNK), jnp.bfloat16),
            pltpu.SemaphoreType.DMA((count, 3)),
        ],
        compiler_params=pltpu.CompilerParams(vmem_limit_bytes=14 << 20),
        cost_estimate=pl.CostEstimate(
            flops=4 * scores * HEAD_DIM,
            bytes_accessed=8 * slots * tokens * CHUNK * count,
            transcendentals=scores,
        ),
    )(position_bias.T, queries, key_rows, values, *after)


def device_index(rep, dp, tensor, dp_size):
    return (rep * dp_size + dp) * 2 + tensor


def ring_order(dp_size):
    half = dp_size // 2
    return [2 * i for i in range(half)] + [2 * i + 1 for i in reversed(range(half))]


def ring_pairs(reps, dp_size, way):
    order = ring_order(dp_size)
    pairs = []
    for rep in range(reps):
        step = way if rep == 0 else -way
        for place in range(dp_size):
            to = order[(place + step) % dp_size]
            for tensor in range(2):
                pairs.append(
                    (
                        device_index(rep, order[place], tensor, dp_size),
                        device_index(rep, to, tensor, dp_size),
                    )
                )
    return pairs


def block_of(distance):
    dp = lax.axis_index("dp")
    place = jnp.where(dp % 2 == 0, dp // 2, 7 - dp // 2)
    way = jnp.where(lax.axis_index("rep") == 0, 1, -1)
    place = (place - way * distance + 16) % 8
    return jnp.where(place < 4, 2 * place, 2 * (7 - place) + 1)


def project_kernel(plan, n_context, n_weights, *refs):
    context = refs[:n_context]
    weights = refs[n_context : n_context + n_weights]
    bases, out_ref = refs[n_context + n_weights : -1], refs[-1]
    for slot, pieces in enumerate(plan):
        total = bases[0][slot] if bases and slot < bases[0].shape[0] else None
        for weight, row, source, column, rows in pieces:
            part = jnp.dot(
                context[source][:, column : column + rows],
                weights[weight][row : row + rows],
                preferred_element_type=jnp.float32,
            )
            total = part if total is None else total + part
        out_ref[slot] = total.astype(out_ref.dtype)


def project(context, weights, plan, kind, bases=()):
    rows = context[0].shape[0]
    depth = sum(piece[-1] for pieces in plan for piece in pieces)
    vmem = pl.BlockSpec(memory_space=pltpu.VMEM)
    return pl.pallas_call(
        functools.partial(project_kernel, plan, len(context), len(weights)),
        out_shape=jax.ShapeDtypeStruct((len(plan), rows, CHUNK), kind),
        in_specs=[vmem] * (len(context) + len(weights) + len(bases)),
        out_specs=vmem,
        compiler_params=pltpu.CompilerParams(vmem_limit_bytes=12 << 20),
        cost_estimate=pl.CostEstimate(
            flops=2 * rows * depth * CHUNK,
            bytes_accessed=2 * (len(plan) * rows * CHUNK + depth * CHUNK),
            transcendentals=0,
        ),
    )(*context, *weights, *bases)


def finish_kernel(distances, counts_ref, donors_ref, *refs):
    n = len(distances)
    kept, other = refs[:n], refs[n : 2 * n]
    out_ref, buffer, sem = refs[-3:]
    slots, tokens = out_ref.shape[:2]
    my_group, tensor = lax.axis_index("dp"), lax.axis_index("tensor")
    second = donors_ref[0] == my_group
    for at in range(1, donors_ref.shape[0]):
        second = jnp.logical_or(second, donors_ref[at] == my_group)
    live = [jnp.where(counts_ref[0] >= 1, 1.0, 0.0), jnp.where(second, 1.0, 0.0)]
    at = 0
    steps = []
    for array, group in enumerate(distances):
        for slot, distance in enumerate(group):
            block = block_of(distance)
            column = pl.multiple_of(block % 4 * CHUNK, CHUNK)
            copy = pltpu.make_async_copy(
                buffer.at[at], out_ref.at[:, :, pl.ds(column, CHUNK)], sem.at[at]
            )
            steps.append((block // 4 == tensor, copy))

            @pl.when(block // 4 == tensor)
            def _():
                for passage in range(slots):
                    rows = slice(passage * tokens, (passage + 1) * tokens)
                    both = kept[array][slot, rows].astype(jnp.float32)
                    both = both + other[array][slot, rows].astype(jnp.float32)
                    buffer[at, passage] = (both * live[passage]).astype(jnp.bfloat16)
                copy.start()

            at += 1
    for mine, copy in steps:

        @pl.when(mine)
        def _():
            copy.wait()


def finish(kept, other, distances, counts, donors, slots, held=()):
    rows = kept[0].shape[1]
    tokens = rows // slots
    smem = pl.BlockSpec(memory_space=pltpu.SMEM)
    vmem = pl.BlockSpec(memory_space=pltpu.VMEM)
    away = pl.BlockSpec(memory_space=pl.ANY)
    blocks = sum(len(group) for group in distances)
    n_in = 2 + 2 * len(kept)
    return pl.pallas_call(
        functools.partial(finish_kernel, distances),
        out_shape=jax.ShapeDtypeStruct((slots, tokens, 4 * CHUNK), jnp.bfloat16),
        in_specs=[smem, smem] + [vmem] * (n_in - 2) + [away] * len(held),
        out_specs=away,
        scratch_shapes=[
            pltpu.VMEM((blocks, slots, tokens, CHUNK), jnp.bfloat16),
            pltpu.SemaphoreType.DMA((blocks,)),
        ],
        input_output_aliases={n_in: 0} if held else {},
        compiler_params=pltpu.CompilerParams(vmem_limit_bytes=12 << 20),
        cost_estimate=pl.CostEstimate(
            flops=blocks * rows * CHUNK,
            bytes_accessed=blocks * rows * CHUNK * 3,
            transcendentals=0,
        ),
    )(counts, donors, *kept, *other, *held)


def with_ring(queries, key_rows, values, position_bias, out_weight, counts, donors, reps, dp_size):
    slots = queries.shape[0]
    ahead = ring_pairs(reps, dp_size, 1)
    back = ring_pairs(reps, dp_size, -1)
    places = [(r, d, t) for r in range(2) for d in range(dp_size) for t in range(2)]
    across = [
        (device_index(r, d, t, dp_size), device_index(1 - r, d, t, dp_size)) for r, d, t in places
    ]
    cores = [
        (device_index(r, d, t, dp_size), device_index(r, d, 1 - t, dp_size)) for r, d, t in places
    ]
    send = lambda value, pairs: lax.ppermute(value, AXES, pairs)
    depth = out_weight.shape[0]
    cut, half = depth // 4, depth // 2
    edge = lambda p, q: jnp.concatenate([p[:cut], q[-cut:]], axis=0)
    barrier = lax.optimization_barrier

    p1, q1 = send(out_weight, ahead), send(out_weight, back)
    c0 = attend(queries, key_rows, values, position_bias, 0, 3)
    p1, q1, c0 = barrier((p1, q1, c0))

    p2, q2 = send(p1[:-cut], ahead), send(q1[cut:], back)
    c1 = attend(queries, key_rows, values, position_bias, 3, 1, (c0,))
    p2, q2, c1 = barrier((p2, q2, c1))
    context = (c0, c1)

    p3, q3, y2 = send(p2, ahead), send(q2, back), send(edge(p2, q2), across)
    whole = lambda w: [(w, 0, 0, 0, 3 * cut), (w, 3 * cut, 1, 0, cut)]
    e1 = project(context, (out_weight, p1, q1), [whole(i) for i in range(3)], jnp.bfloat16)
    p3, q3, y2, e1 = barrier((p3, q3, y2, e1))

    p4, q4 = send(p3[:half], ahead), send(q3[-half:], back)
    y3 = send(edge(p3, q3), across)
    x1 = send(e1, cores)
    p_part = lambda w: [(w, 0, 0, 0, 3 * cut)]
    q_part = lambda w: [(w, 0, 0, cut, 2 * cut), (w, 2 * cut, 1, 0, cut)]
    p_rest = lambda w: [(w, cut, 1, 0, cut)]
    q_rest = lambda w: [(w, 0, 0, 0, cut)]
    e2 = project(
        context, (p2, q2, y2), [p_part(0) + p_rest(2), q_part(1) + q_rest(2)], jnp.bfloat16
    )
    started = project(context, (p3, q3), [p_part(0), q_part(1)], jnp.float32)
    p4, q4, y3, e2, x1, started = barrier((p4, q4, y3, e2, x1, started))

    x2 = send(e2, cores)
    opposite = [(1, 0, 0, 0, half), (2, 0, 0, half, cut), (2, cut, 1, 0, cut)]
    e3 = project(
        context, (y3, p4, q4), [p_rest(0), q_rest(0), opposite], jnp.bfloat16, (started,)
    )
    x3 = send(e3, cores)
    early = finish((e1, e2), (x1, x2), ((0, 1, -1), (2, -2)), counts, donors, slots)
    x3, early = barrier((x3, early))
    return finish((e3,), (x3,), ((3, -3, 4),), counts, donors, slots, (early,))


def with_gather(queries, key_rows, values, position_bias, out_weight, counts, donors):
    slots, tokens, features = queries.shape
    whole = lax.all_gather(out_weight, "dp", axis=1, tiled=True)
    context = attend(queries, key_rows, values, position_bias, 0, features // CHUNK)
    product = jnp.dot(context, whole, preferred_element_type=jnp.float32).astype(jnp.bfloat16)
    merged = lax.psum_scatter(product, "tensor", scatter_dimension=1, tiled=True)
    first_live = counts[0] >= 1
    second_live = jnp.any(donors == lax.axis_index("dp"))
    live = jnp.stack([first_live, second_live]).astype(jnp.bfloat16)
    return merged.reshape(slots, tokens, merged.shape[1]) * live[:, None, None]


def solution(mesh):
    in_specs = (
        P(("rep", "dp"), None, "tensor"),
        P(("rep", "dp"), None, "tensor"),
        P(("rep", "dp"), None, "tensor"),
        P(None, "tensor"),
        P("tensor", "dp"),
        P(("rep", "dp")),
        P("rep"),
    )
    out_specs = P(("rep", "dp"), None, "tensor")
    reps, dp_size = mesh.shape["rep"], mesh.shape["dp"]
    if reps == 2 and dp_size == 8 and mesh.shape["tensor"] == 2:
        on_device = functools.partial(with_ring, reps=reps, dp_size=dp_size)
    else:
        on_device = with_gather
    return jax.shard_map(
        on_device, mesh=mesh, in_specs=in_specs, out_specs=out_specs, check_vma=False
    )
```

```python
import functools

import jax
import jax.numpy as jnp
from jax import lax
from jax.experimental import pallas as pl
from jax.experimental.pallas import tpu as pltpu
from jax.sharding import PartitionSpec as P

HEAD_DIM = 64
PAIR = 2 * HEAD_DIM
CHUNK = 256
THRESHOLDS = (12, 16, 23, 32, 46, 64, 91)
AXES = ("rep", "dp", "tensor")


def bias_rows(position_bias, tokens):
    bucket_count = position_bias.shape[1]
    shape = (bucket_count, 2 * tokens)
    relative = lax.broadcasted_iota(jnp.int32, shape, 1) - (tokens - 1)
    distance = jnp.abs(relative)
    far = jnp.full(shape, 8, jnp.int32)
    for threshold in THRESHOLDS:
        far = far + jnp.where(distance >= threshold, 1, 0)
    bucket = jnp.where(distance < 8, distance, far) + jnp.where(relative > 0, 16, 0)
    one_hot = jnp.where(bucket == lax.broadcasted_iota(jnp.int32, shape, 0), 1.0, 0.0)
    return lax.dot_general(
        position_bias,
        one_hot,
        (((1,), (0,)), ((), ())),
        precision=lax.Precision.HIGHEST,
        preferred_element_type=jnp.float32,
    )


def attention_kernel(first, bias_ref, *refs):
    sources, (out_ref, held, sem) = refs[:3], refs[-3:]
    count, _, slots, tokens, width = held.shape
    copies = [
        [
            pltpu.make_async_copy(
                source.at[:, :, (first + chunk) * width : (first + chunk + 1) * width],
                held.at[chunk, at],
                sem.at[chunk, at],
            )
            for at, source in enumerate(sources)
        ]
        for chunk in range(count)
    ]
    for chunk in copies:
        for copy in chunk:
            copy.start()
    rows = bias_rows(bias_ref[...], tokens)
    lower = lax.broadcasted_iota(jnp.int32, (tokens, PAIR), 1) < HEAD_DIM
    for chunk in range(count):
        for copy in copies[chunk]:
            copy.wait()
        for pair in range(width // PAIR):
            columns = slice(pair * PAIR, (pair + 1) * PAIR)
            head = (first + chunk) * (width // HEAD_DIM) + 2 * pair
            terms = [toeplitz(rows[head + i : head + i + 1], tokens) for i in range(2)]
            for slot in range(slots):
                query, key, value = (held[chunk, at, slot, :, columns] for at in range(3))
                sums = []
                for i in range(2):
                    own = lower if i == 0 else jnp.logical_not(lower)
                    scores = lax.dot_general(
                        query,
                        jnp.where(own, key, 0),
                        (((1,), (1,)), ((), ())),
                        preferred_element_type=jnp.float32,
                    )
                    scores = scores + terms[i]
                    highest = jnp.max(scores, axis=-1, keepdims=True)
                    expd = jnp.exp(scores - highest).astype(jnp.bfloat16)
                    sums.append(
                        jnp.dot(expd, jnp.where(own, value, 1), preferred_element_type=jnp.float32)
                    )
                weighted = jnp.where(lower, sums[0], sums[1])
                total = pltpu.roll(jnp.where(lower, sums[1], sums[0]), HEAD_DIM, 1)
                at = slice(chunk * width + pair * PAIR, chunk * width + (pair + 1) * PAIR)
                out_ref[slot * tokens : (slot + 1) * tokens, at] = (weighted / total).astype(
                    jnp.bfloat16
                )


def toeplitz(row, tokens):
    spread = jnp.broadcast_to(row, (8, 2 * tokens))
    base = pltpu.roll(spread, tokens + 1, 1, stride=1, stride_axis=0)
    rolled = [base if i == 0 else pltpu.roll(base, 8 * i, 1) for i in range(16)]
    groups = []
    for group in range(tokens // 8):
        turned, whole = rolled[group % 16], group // 16 * 128
        if whole:
            turned = jnp.concatenate([turned[:, -whole:], turned[:, : tokens - whole]], axis=1)
        groups.append(turned[:, :tokens])
    return jnp.concatenate(groups, axis=0)


def attend(queries, key_rows, values, position_bias, first, count, after=()):
    slots, tokens, _ = queries.shape
    vmem = pl.BlockSpec(memory_space=pltpu.VMEM)
    away = pl.BlockSpec(memory_space=pltpu.HBM)
    scores = slots * (CHUNK // HEAD_DIM) * tokens * tokens * count
    return pl.pallas_call(
        functools.partial(attention_kernel, first),
        out_shape=jax.ShapeDtypeStruct((slots * tokens, CHUNK * count), jnp.bfloat16),
        in_specs=[vmem] + [away] * 3 + [pl.BlockSpec(memory_space=pl.ANY)] * len(after),
        out_specs=vmem,
        scratch_shapes=[
            pltpu.VMEM((count, 3, slots, tokens, CHUNK), jnp.bfloat16),
            pltpu.SemaphoreType.DMA((count, 3)),
        ],
        compiler_params=pltpu.CompilerParams(vmem_limit_bytes=14 << 20),
        cost_estimate=pl.CostEstimate(
            flops=4 * scores * HEAD_DIM,
            bytes_accessed=8 * slots * tokens * CHUNK * count,
            transcendentals=scores,
        ),
    )(position_bias.T, queries, key_rows, values, *after)


def device_index(rep, dp, tensor, dp_size):
    return (rep * dp_size + dp) * 2 + tensor


def ring_order(dp_size):
    half = dp_size // 2
    return [2 * i for i in range(half)] + [2 * i + 1 for i in reversed(range(half))]


def ring_pairs(reps, dp_size, way):
    order = ring_order(dp_size)
    pairs = []
    for rep in range(reps):
        step = way if rep == 0 else -way
        for place in range(dp_size):
            to = order[(place + step) % dp_size]
            for tensor in range(2):
                pairs.append(
                    (
                        device_index(rep, order[place], tensor, dp_size),
                        device_index(rep, to, tensor, dp_size),
                    )
                )
    return pairs


def block_of(distance):
    dp = lax.axis_index("dp")
    place = jnp.where(dp % 2 == 0, dp // 2, 7 - dp // 2)
    way = jnp.where(lax.axis_index("rep") == 0, 1, -1)
    place = (place - way * distance + 16) % 8
    return jnp.where(place < 4, 2 * place, 2 * (7 - place) + 1)


def project_kernel(plan, n_context, n_weights, *refs):
    context = refs[:n_context]
    weights = refs[n_context : n_context + n_weights]
    bases, out_ref = refs[n_context + n_weights : -1], refs[-1]
    for slot, pieces in enumerate(plan):
        total = bases[0][slot] if bases and slot < bases[0].shape[0] else None
        for weight, row, source, column, rows in pieces:
            part = jnp.dot(
                context[source][:, column : column + rows],
                weights[weight][row : row + rows],
                preferred_element_type=jnp.float32,
            )
            total = part if total is None else total + part
        out_ref[slot] = total.astype(out_ref.dtype)


def project(context, weights, plan, kind, bases=()):
    rows = context[0].shape[0]
    depth = sum(piece[-1] for pieces in plan for piece in pieces)
    vmem = pl.BlockSpec(memory_space=pltpu.VMEM)
    return pl.pallas_call(
        functools.partial(project_kernel, plan, len(context), len(weights)),
        out_shape=jax.ShapeDtypeStruct((len(plan), rows, CHUNK), kind),
        in_specs=[vmem] * (len(context) + len(weights) + len(bases)),
        out_specs=vmem,
        compiler_params=pltpu.CompilerParams(vmem_limit_bytes=12 << 20),
        cost_estimate=pl.CostEstimate(
            flops=2 * rows * depth * CHUNK,
            bytes_accessed=2 * (len(plan) * rows * CHUNK + depth * CHUNK),
            transcendentals=0,
        ),
    )(*context, *weights, *bases)


def finish_kernel(distances, counts_ref, donors_ref, *refs):
    n = len(distances)
    kept, other = refs[:n], refs[n : 2 * n]
    out_ref, buffer, sem = refs[-3:]
    slots, tokens = out_ref.shape[:2]
    my_group, tensor = lax.axis_index("dp"), lax.axis_index("tensor")
    second = donors_ref[0] == my_group
    for at in range(1, donors_ref.shape[0]):
        second = jnp.logical_or(second, donors_ref[at] == my_group)
    live = [jnp.where(counts_ref[0] >= 1, 1.0, 0.0), jnp.where(second, 1.0, 0.0)]
    at = 0
    steps = []
    for array, group in enumerate(distances):
        for slot, distance in enumerate(group):
            block = block_of(distance)
            column = pl.multiple_of(block % 4 * CHUNK, CHUNK)
            copy = pltpu.make_async_copy(
                buffer.at[at], out_ref.at[:, :, pl.ds(column, CHUNK)], sem.at[at]
            )
            steps.append((block // 4 == tensor, copy))

            @pl.when(block // 4 == tensor)
            def _():
                for passage in range(slots):
                    rows = slice(passage * tokens, (passage + 1) * tokens)
                    both = kept[array][slot, rows].astype(jnp.float32)
                    both = both + other[array][slot, rows].astype(jnp.float32)
                    buffer[at, passage] = (both * live[passage]).astype(jnp.bfloat16)
                copy.start()

            at += 1
    for mine, copy in steps:

        @pl.when(mine)
        def _():
            copy.wait()


def finish(kept, other, distances, counts, donors, slots, held=()):
    rows = kept[0].shape[1]
    tokens = rows // slots
    smem = pl.BlockSpec(memory_space=pltpu.SMEM)
    vmem = pl.BlockSpec(memory_space=pltpu.VMEM)
    away = pl.BlockSpec(memory_space=pl.ANY)
    blocks = sum(len(group) for group in distances)
    n_in = 2 + 2 * len(kept)
    return pl.pallas_call(
        functools.partial(finish_kernel, distances),
        out_shape=jax.ShapeDtypeStruct((slots, tokens, 4 * CHUNK), jnp.bfloat16),
        in_specs=[smem, smem] + [vmem] * (n_in - 2) + [away] * len(held),
        out_specs=away,
        scratch_shapes=[
            pltpu.VMEM((blocks, slots, tokens, CHUNK), jnp.bfloat16),
            pltpu.SemaphoreType.DMA((blocks,)),
        ],
        input_output_aliases={n_in: 0} if held else {},
        compiler_params=pltpu.CompilerParams(vmem_limit_bytes=12 << 20),
        cost_estimate=pl.CostEstimate(
            flops=blocks * rows * CHUNK,
            bytes_accessed=blocks * rows * CHUNK * 3,
            transcendentals=0,
        ),
    )(counts, donors, *kept, *other, *held)


def with_ring(queries, key_rows, values, position_bias, out_weight, counts, donors, reps, dp_size):
    slots = queries.shape[0]
    ahead = ring_pairs(reps, dp_size, 1)
    back = ring_pairs(reps, dp_size, -1)
    places = [(r, d, t) for r in range(2) for d in range(dp_size) for t in range(2)]
    across = [
        (device_index(r, d, t, dp_size), device_index(1 - r, d, t, dp_size)) for r, d, t in places
    ]
    cores = [
        (device_index(r, d, t, dp_size), device_index(r, d, 1 - t, dp_size)) for r, d, t in places
    ]
    send = lambda value, pairs: lax.ppermute(value, AXES, pairs)
    depth = out_weight.shape[0]
    cut, half = 3 * depth // 8, depth // 2
    over = half - cut
    edge = lambda p, q: jnp.concatenate([p[:cut], q[-cut:]], axis=0)
    barrier = lax.optimization_barrier

    upper, lower = out_weight[:-cut], out_weight[cut:]
    p1, q1 = send(upper, ahead), send(lower, back)
    c0 = attend(queries, key_rows, values, position_bias, 0, 2)
    p1, q1, c0 = barrier((p1, q1, c0))

    y1 = send(edge(p1, q1), across)
    p2, q2 = send(p1, ahead), send(q1, back)
    c1 = attend(queries, key_rows, values, position_bias, 2, 2, (c0,))
    p2, q2, y1, c1 = barrier((p2, q2, y1, c1))
    context = (c0, c1)
    p_part = lambda w: [(w, 0, 0, 0, half), (w, half, 1, 0, over)]
    q_part = lambda w: [(w, 0, 0, cut, over), (w, over, 1, 0, half)]
    p_rest = lambda w: [(w, cut, 1, over, cut)]
    q_rest = lambda w: [(w, 0, 0, 0, cut)]
    pair = lambda p, q, y: [p_part(p) + p_rest(y), q_part(q) + q_rest(y)]
    own = [(0, 0, 0, 0, half), (0, half, 1, 0, half)]

    y2 = send(edge(p2, q2), across)
    p3, q3 = send(p2, ahead), send(q2, back)
    e1 = project(context, (out_weight, p1, q1, y1), [own] + pair(1, 2, 3), jnp.bfloat16)
    p3, q3, y2, e1 = barrier((p3, q3, y2, e1))

    y3 = send(edge(p3, q3), across)
    p4, q4 = send(p3[:half], ahead), send(q3[-half:], back)
    e2 = project(context, (p2, q2, y2), pair(0, 1, 2), jnp.bfloat16)
    started = project(context, (p3, q3), [p_part(0), q_part(1)], jnp.float32)
    p4, q4, y3, e1, e2, started = barrier((p4, q4, y3, e1, e2, started))

    x1, x2 = send(e1, cores), send(e2, cores)
    opposite = [(1, 0, 0, 0, half), (2, 0, 1, 0, half)]
    e3 = project(
        context, (y3, p4, q4), [p_rest(0), q_rest(0), opposite], jnp.bfloat16, (started,)
    )
    x3 = send(e3, cores)
    early = finish((e1,), (x1,), ((0, 1, -1),), counts, donors, slots)
    x2, x3, early = barrier((x2, x3, early))
    return finish((e2, e3), (x2, x3), ((2, -2), (3, -3, 4)), counts, donors, slots, (early,))


def with_gather(queries, key_rows, values, position_bias, out_weight, counts, donors):
    slots, tokens, features = queries.shape
    whole = lax.all_gather(out_weight, "dp", axis=1, tiled=True)
    context = attend(queries, key_rows, values, position_bias, 0, features // CHUNK)
    product = jnp.dot(context, whole, preferred_element_type=jnp.float32).astype(jnp.bfloat16)
    merged = lax.psum_scatter(product, "tensor", scatter_dimension=1, tiled=True)
    first_live = counts[0] >= 1
    second_live = jnp.any(donors == lax.axis_index("dp"))
    live = jnp.stack([first_live, second_live]).astype(jnp.bfloat16)
    return merged.reshape(slots, tokens, merged.shape[1]) * live[:, None, None]


def solution(mesh):
    in_specs = (
        P(("rep", "dp"), None, "tensor"),
        P(("rep", "dp"), None, "tensor"),
        P(("rep", "dp"), None, "tensor"),
        P(None, "tensor"),
        P("tensor", "dp"),
        P(("rep", "dp")),
        P("rep"),
    )
    out_specs = P(("rep", "dp"), None, "tensor")
    reps, dp_size = mesh.shape["rep"], mesh.shape["dp"]
    if reps == 2 and dp_size == 8 and mesh.shape["tensor"] == 2:
        on_device = functools.partial(with_ring, reps=reps, dp_size=dp_size)
    else:
        on_device = with_gather
    return jax.shard_map(
        on_device, mesh=mesh, in_specs=in_specs, out_specs=out_specs, check_vma=False
    )
```

```python
import functools

import jax
import jax.numpy as jnp
from jax import lax
from jax.experimental import pallas as pl
from jax.experimental.pallas import tpu as pltpu
from jax.sharding import PartitionSpec as P

HEAD_DIM = 64
PAIR = 2 * HEAD_DIM
CHUNK = 256
THRESHOLDS = (12, 16, 23, 32, 46, 64, 91)
AXES = ("rep", "dp", "tensor")


def bias_rows(position_bias, tokens):
    bucket_count = position_bias.shape[1]
    shape = (bucket_count, 2 * tokens)
    relative = lax.broadcasted_iota(jnp.int32, shape, 1) - (tokens - 1)
    distance = jnp.abs(relative)
    far = jnp.full(shape, 8, jnp.int32)
    for threshold in THRESHOLDS:
        far = far + jnp.where(distance >= threshold, 1, 0)
    bucket = jnp.where(distance < 8, distance, far) + jnp.where(relative > 0, 16, 0)
    one_hot = jnp.where(bucket == lax.broadcasted_iota(jnp.int32, shape, 0), 1.0, 0.0)
    return lax.dot_general(
        position_bias,
        one_hot,
        (((1,), (0,)), ((), ())),
        precision=lax.Precision.HIGHEST,
        preferred_element_type=jnp.float32,
    )


def attention_kernel(first, bias_ref, *refs):
    sources, (out_ref, held, sem) = refs[:3], refs[-3:]
    count, _, slots, tokens, width = held.shape
    copies = [
        [
            pltpu.make_async_copy(
                source.at[:, :, (first + chunk) * width : (first + chunk + 1) * width],
                held.at[chunk, at],
                sem.at[chunk, at],
            )
            for at, source in enumerate(sources)
        ]
        for chunk in range(count)
    ]
    for chunk in copies:
        for copy in chunk:
            copy.start()
    rows = bias_rows(bias_ref[...], tokens)
    lower = lax.broadcasted_iota(jnp.int32, (tokens, PAIR), 1) < HEAD_DIM
    for chunk in range(count):
        for copy in copies[chunk]:
            copy.wait()
        for pair in range(width // PAIR):
            columns = slice(pair * PAIR, (pair + 1) * PAIR)
            head = (first + chunk) * (width // HEAD_DIM) + 2 * pair
            terms = [toeplitz(rows[head + i : head + i + 1], tokens) for i in range(2)]
            for slot in range(slots):
                query, key, value = (held[chunk, at, slot, :, columns] for at in range(3))
                sums = []
                for i in range(2):
                    own = lower if i == 0 else jnp.logical_not(lower)
                    scores = lax.dot_general(
                        query,
                        jnp.where(own, key, 0),
                        (((1,), (1,)), ((), ())),
                        preferred_element_type=jnp.float32,
                    )
                    scores = scores + terms[i]
                    highest = jnp.max(scores, axis=-1, keepdims=True)
                    expd = jnp.exp(scores - highest).astype(jnp.bfloat16)
                    sums.append(
                        jnp.dot(expd, jnp.where(own, value, 1), preferred_element_type=jnp.float32)
                    )
                weighted = jnp.where(lower, sums[0], sums[1])
                total = pltpu.roll(jnp.where(lower, sums[1], sums[0]), HEAD_DIM, 1)
                at = slice(chunk * width + pair * PAIR, chunk * width + (pair + 1) * PAIR)
                out_ref[slot * tokens : (slot + 1) * tokens, at] = (weighted / total).astype(
                    jnp.bfloat16
                )


def toeplitz(row, tokens):
    spread = jnp.broadcast_to(row, (8, 2 * tokens))
    base = pltpu.roll(spread, tokens + 1, 1, stride=1, stride_axis=0)
    rolled = [base if i == 0 else pltpu.roll(base, 8 * i, 1) for i in range(16)]
    groups = []
    for group in range(tokens // 8):
        turned, whole = rolled[group % 16], group // 16 * 128
        if whole:
            turned = jnp.concatenate([turned[:, -whole:], turned[:, : tokens - whole]], axis=1)
        groups.append(turned[:, :tokens])
    return jnp.concatenate(groups, axis=0)


def attend(queries, key_rows, values, position_bias, first, count, after=()):
    slots, tokens, _ = queries.shape
    vmem = pl.BlockSpec(memory_space=pltpu.VMEM)
    away = pl.BlockSpec(memory_space=pltpu.HBM)
    scores = slots * (CHUNK // HEAD_DIM) * tokens * tokens * count
    return pl.pallas_call(
        functools.partial(attention_kernel, first),
        out_shape=jax.ShapeDtypeStruct((slots * tokens, CHUNK * count), jnp.bfloat16),
        in_specs=[vmem] + [away] * 3 + [pl.BlockSpec(memory_space=pl.ANY)] * len(after),
        out_specs=vmem,
        scratch_shapes=[
            pltpu.VMEM((count, 3, slots, tokens, CHUNK), jnp.bfloat16),
            pltpu.SemaphoreType.DMA((count, 3)),
        ],
        compiler_params=pltpu.CompilerParams(vmem_limit_bytes=14 << 20),
        cost_estimate=pl.CostEstimate(
            flops=4 * scores * HEAD_DIM,
            bytes_accessed=8 * slots * tokens * CHUNK * count,
            transcendentals=scores,
        ),
    )(position_bias.T, queries, key_rows, values, *after)


def device_index(rep, dp, tensor, dp_size):
    return (rep * dp_size + dp) * 2 + tensor


def ring_order(dp_size):
    half = dp_size // 2
    return [2 * i for i in range(half)] + [2 * i + 1 for i in reversed(range(half))]


def ring_pairs(reps, dp_size, way):
    order = ring_order(dp_size)
    pairs = []
    for rep in range(reps):
        step = way if rep == 0 else -way
        for place in range(dp_size):
            to = order[(place + step) % dp_size]
            for tensor in range(2):
                pairs.append(
                    (
                        device_index(rep, order[place], tensor, dp_size),
                        device_index(rep, to, tensor, dp_size),
                    )
                )
    return pairs


def block_of(distance):
    dp = lax.axis_index("dp")
    place = jnp.where(dp % 2 == 0, dp // 2, 7 - dp // 2)
    way = jnp.where(lax.axis_index("rep") == 0, 1, -1)
    place = (place - way * distance + 16) % 8
    return jnp.where(place < 4, 2 * place, 2 * (7 - place) + 1)


def project_kernel(plan, n_context, n_weights, *refs):
    context = refs[:n_context]
    weights = refs[n_context : n_context + n_weights]
    bases, out_ref = refs[n_context + n_weights : -1], refs[-1]
    for slot, products in enumerate(plan):
        total = bases[0][slot] if bases and slot < bases[0].shape[0] else None
        for source, column, pieces in products:
            parts = [weights[weight][row : row + rows] for weight, row, rows in pieces]
            rows = parts[0] if len(parts) == 1 else jnp.concatenate(parts, axis=0)
            part = jnp.dot(
                context[source][:, column : column + rows.shape[0]],
                rows,
                preferred_element_type=jnp.float32,
            )
            total = part if total is None else total + part
        out_ref[slot] = total.astype(out_ref.dtype)


def project(context, weights, plan, kind, bases=()):
    rows = context[0].shape[0]
    depth = sum(piece[-1] for block in plan for product in block for piece in product[-1])
    vmem = pl.BlockSpec(memory_space=pltpu.VMEM)
    return pl.pallas_call(
        functools.partial(project_kernel, plan, len(context), len(weights)),
        out_shape=jax.ShapeDtypeStruct((len(plan), rows, CHUNK), kind),
        in_specs=[vmem] * (len(context) + len(weights) + len(bases)),
        out_specs=vmem,
        compiler_params=pltpu.CompilerParams(vmem_limit_bytes=12 << 20),
        cost_estimate=pl.CostEstimate(
            flops=2 * rows * depth * CHUNK,
            bytes_accessed=2 * (len(plan) * rows * CHUNK + depth * CHUNK),
            transcendentals=0,
        ),
    )(*context, *weights, *bases)


def finish_kernel(distances, counts_ref, donors_ref, *refs):
    n = len(distances)
    kept, other = refs[:n], refs[n : 2 * n]
    out_ref, buffer, sem = refs[-3:]
    slots, tokens = out_ref.shape[:2]
    my_group, tensor = lax.axis_index("dp"), lax.axis_index("tensor")
    second = donors_ref[0] == my_group
    for at in range(1, donors_ref.shape[0]):
        second = jnp.logical_or(second, donors_ref[at] == my_group)
    live = [
        jnp.where(lives, 1.0, 0.0).astype(jnp.bfloat16) for lives in (counts_ref[0] >= 1, second)
    ]
    at = 0
    steps = []
    for array, group in enumerate(distances):
        for slot, distance in enumerate(group):
            block = block_of(distance)
            column = pl.multiple_of(block % 4 * CHUNK, CHUNK)
            copy = pltpu.make_async_copy(
                buffer.at[at], out_ref.at[:, :, pl.ds(column, CHUNK)], sem.at[at]
            )
            steps.append((block // 4 == tensor, copy))

            @pl.when(block // 4 == tensor)
            def _():
                for passage in range(slots):
                    rows = slice(passage * tokens, (passage + 1) * tokens)
                    both = kept[array][slot, rows] + other[array][slot, rows]
                    buffer[at, passage] = both * live[passage]
                copy.start()

            at += 1
    for mine, copy in steps:

        @pl.when(mine)
        def _():
            copy.wait()


def finish(kept, other, distances, counts, donors, slots, held=()):
    rows = kept[0].shape[1]
    tokens = rows // slots
    smem = pl.BlockSpec(memory_space=pltpu.SMEM)
    vmem = pl.BlockSpec(memory_space=pltpu.VMEM)
    away = pl.BlockSpec(memory_space=pl.ANY)
    blocks = sum(len(group) for group in distances)
    n_in = 2 + 2 * len(kept)
    return pl.pallas_call(
        functools.partial(finish_kernel, distances),
        out_shape=jax.ShapeDtypeStruct((slots, tokens, 4 * CHUNK), jnp.bfloat16),
        in_specs=[smem, smem] + [vmem] * (n_in - 2) + [away] * len(held),
        out_specs=away,
        scratch_shapes=[
            pltpu.VMEM((blocks, slots, tokens, CHUNK), jnp.bfloat16),
            pltpu.SemaphoreType.DMA((blocks,)),
        ],
        input_output_aliases={n_in: 0} if held else {},
        compiler_params=pltpu.CompilerParams(vmem_limit_bytes=12 << 20),
        cost_estimate=pl.CostEstimate(
            flops=blocks * rows * CHUNK,
            bytes_accessed=blocks * rows * CHUNK * 3,
            transcendentals=0,
        ),
    )(counts, donors, *kept, *other, *held)


def with_ring(queries, key_rows, values, position_bias, out_weight, counts, donors, reps, dp_size):
    slots = queries.shape[0]
    ahead = ring_pairs(reps, dp_size, 1)
    back = ring_pairs(reps, dp_size, -1)
    places = [(r, d, t) for r in range(2) for d in range(dp_size) for t in range(2)]
    across = [
        (device_index(r, d, t, dp_size), device_index(1 - r, d, t, dp_size)) for r, d, t in places
    ]
    cores = [
        (device_index(r, d, t, dp_size), device_index(r, d, 1 - t, dp_size)) for r, d, t in places
    ]
    send = lambda value, pairs: lax.ppermute(value, AXES, pairs)
    depth = out_weight.shape[0]
    half, cut = depth // 2, 11 * depth // 32
    over = half - cut
    lead = over // 128 * 128
    spill = over - lead
    edge = lambda p, q: jnp.concatenate([p[:cut], q[-cut:]], axis=0)
    barrier = lax.optimization_barrier

    p1, q1 = send(out_weight[:-cut], ahead), send(out_weight[cut:], back)
    c0 = attend(queries, key_rows, values, position_bias, 0, 2)
    p1, c0 = barrier((p1, c0))

    p2, q2, y1 = send(p1, ahead), send(q1, back), send(edge(p1, q1), across)
    c1 = attend(queries, key_rows, values, position_bias, 2, 2, (c0,))
    p2, c1 = barrier((p2, c1))
    context = (c0, c1)

    p3, q3, y2 = send(p2, ahead), send(q2, back), send(edge(p2, q2), across)
    p3, q3, y1 = barrier((p3, q3, y1))

    own = [(0, 0, [(0, 0, half)]), (1, 0, [(0, half, half)])]
    p_block = lambda p, y: [(0, 0, [(p, 0, half)]), (1, 0, [(p, half, over), (y, cut, cut)])]
    q_block = lambda q, y: [(0, 0, [(y, 0, cut), (q, 0, over)]), (1, 0, [(q, over, half)])]
    p_part = [(0, 0, [(0, 0, half)]), (1, 0, [(0, half, lead)])]
    q_part = [(0, half - lead, [(1, spill, lead)]), (1, 0, [(1, over, half)])]
    p_rest = [(1, lead, [(0, half + lead, spill), (2, cut, cut)])]
    q_rest = [(0, 0, [(2, 0, cut), (1, 0, spill)])]
    opposite = [(0, 0, [(3, 0, half)]), (1, 0, [(4, 0, half)])]

    p4, q4 = send(p3[:half], ahead), send(q3[-half:], back)
    y3 = send(edge(p3, q3), across)
    e1 = project(
        context, (out_weight, p1, q1, y1), [own, p_block(1, 3), q_block(2, 3)], jnp.bfloat16
    )
    e2 = project(context, (p2, q2, y2), [p_block(0, 2), q_block(1, 2)], jnp.bfloat16)
    started = project(context, (p3, q3), [p_part, q_part], jnp.float32)
    p4, q4, y3, e1, e2, started = barrier((p4, q4, y3, e1, e2, started))

    x1, x2 = send(e1, cores), send(e2, cores)
    e3 = project(
        context, (p3, q3, y3, p4, q4), [p_rest, q_rest, opposite], jnp.bfloat16, (started,)
    )
    x3 = send(e3, cores)
    early = finish((e1,), (x1,), ((0, 1, -1),), counts, donors, slots)
    x2, x3, early = barrier((x2, x3, early))
    return finish((e2, e3), (x2, x3), ((2, -2), (3, -3, 4)), counts, donors, slots, (early,))


def with_gather(queries, key_rows, values, position_bias, out_weight, counts, donors):
    slots, tokens, features = queries.shape
    whole = lax.all_gather(out_weight, "dp", axis=1, tiled=True)
    context = attend(queries, key_rows, values, position_bias, 0, features // CHUNK)
    product = jnp.dot(context, whole, preferred_element_type=jnp.float32).astype(jnp.bfloat16)
    merged = lax.psum_scatter(product, "tensor", scatter_dimension=1, tiled=True)
    first_live = counts[0] >= 1
    second_live = jnp.any(donors == lax.axis_index("dp"))
    live = jnp.stack([first_live, second_live]).astype(jnp.bfloat16)
    return merged.reshape(slots, tokens, merged.shape[1]) * live[:, None, None]


def solution(mesh):
    in_specs = (
        P(("rep", "dp"), None, "tensor"),
        P(("rep", "dp"), None, "tensor"),
        P(("rep", "dp"), None, "tensor"),
        P(None, "tensor"),
        P("tensor", "dp"),
        P(("rep", "dp")),
        P("rep"),
    )
    out_specs = P(("rep", "dp"), None, "tensor")
    reps, dp_size = mesh.shape["rep"], mesh.shape["dp"]
    if reps == 2 and dp_size == 8 and mesh.shape["tensor"] == 2:
        on_device = functools.partial(with_ring, reps=reps, dp_size=dp_size)
    else:
        on_device = with_gather
    return jax.shard_map(
        on_device, mesh=mesh, in_specs=in_specs, out_specs=out_specs, check_vma=False
    )
```

```python
import functools

import jax
import jax.numpy as jnp
from jax import lax
from jax.experimental import pallas as pl
from jax.experimental.pallas import tpu as pltpu
from jax.sharding import PartitionSpec as P

HEAD_DIM = 64
PAIR = 2 * HEAD_DIM
CHUNK = 256
THRESHOLDS = (12, 16, 23, 32, 46, 64, 91)
AXES = ("rep", "dp", "tensor")


def bias_rows(position_bias, tokens):
    bucket_count = position_bias.shape[1]
    shape = (bucket_count, 2 * tokens)
    relative = lax.broadcasted_iota(jnp.int32, shape, 1) - (tokens - 1)
    distance = jnp.abs(relative)
    far = jnp.full(shape, 8, jnp.int32)
    for threshold in THRESHOLDS:
        far = far + jnp.where(distance >= threshold, 1, 0)
    bucket = jnp.where(distance < 8, distance, far) + jnp.where(relative > 0, 16, 0)
    one_hot = jnp.where(bucket == lax.broadcasted_iota(jnp.int32, shape, 0), 1.0, 0.0)
    return lax.dot_general(
        position_bias,
        one_hot,
        (((1,), (0,)), ((), ())),
        precision=lax.Precision.HIGHEST,
        preferred_element_type=jnp.float32,
    )


def attention_kernel(first, bias_ref, *refs):
    sources, (out_ref, held, sem, counts_ref, donors_ref, live_sem) = refs[:3], refs[-6:]
    live_copies = [
        pltpu.make_async_copy(source, target, live_sem.at[at])
        for at, (source, target) in enumerate(zip(refs[3:5], (counts_ref, donors_ref)))
    ]
    for copy in live_copies:
        copy.start()
    count, _, slots, tokens, width = held.shape
    copies = [
        [
            pltpu.make_async_copy(
                source.at[:, :, (first + chunk) * width : (first + chunk + 1) * width],
                held.at[chunk, at],
                sem.at[chunk, at],
            )
            for at, source in enumerate(sources)
        ]
        for chunk in range(count)
    ]
    for chunk in copies:
        for copy in chunk:
            copy.start()
    rows = bias_rows(bias_ref[...], tokens)
    lower = lax.broadcasted_iota(jnp.int32, (tokens, PAIR), 1) < HEAD_DIM
    for copy in live_copies:
        copy.wait()
    my_group = lax.axis_index("dp")
    second = donors_ref[0] == my_group
    for at in range(1, donors_ref.shape[0]):
        second = jnp.logical_or(second, donors_ref[at] == my_group)
    live = [jnp.where(lives, 1.0, 0.0) for lives in (counts_ref[0] >= 1, second)]
    for chunk in range(count):
        for copy in copies[chunk]:
            copy.wait()
        for pair in range(width // PAIR):
            columns = slice(pair * PAIR, (pair + 1) * PAIR)
            head = (first + chunk) * (width // HEAD_DIM) + 2 * pair
            terms = [toeplitz(rows[head + i : head + i + 1], tokens) for i in range(2)]
            for slot in range(slots):
                query, key, value = (held[chunk, at, slot, :, columns] for at in range(3))
                sums = []
                for i in range(2):
                    own = lower if i == 0 else jnp.logical_not(lower)
                    scores = lax.dot_general(
                        query,
                        jnp.where(own, key, 0),
                        (((1,), (1,)), ((), ())),
                        preferred_element_type=jnp.float32,
                    )
                    scores = scores + terms[i]
                    highest = jnp.max(scores, axis=-1, keepdims=True)
                    expd = jnp.exp(scores - highest).astype(jnp.bfloat16)
                    sums.append(
                        jnp.dot(expd, jnp.where(own, value, 1), preferred_element_type=jnp.float32)
                    )
                weighted = jnp.where(lower, sums[0], sums[1])
                total = pltpu.roll(jnp.where(lower, sums[1], sums[0]), HEAD_DIM, 1)
                at = slice(chunk * width + pair * PAIR, chunk * width + (pair + 1) * PAIR)
                out_ref[slot * tokens : (slot + 1) * tokens, at] = (
                    weighted / total * live[slot]
                ).astype(jnp.bfloat16)


def toeplitz(row, tokens):
    spread = jnp.broadcast_to(row, (8, 2 * tokens))
    base = pltpu.roll(spread, tokens + 1, 1, stride=1, stride_axis=0)
    rolled = [base if i == 0 else pltpu.roll(base, 8 * i, 1) for i in range(16)]
    groups = []
    for group in range(tokens // 8):
        turned, whole = rolled[group % 16], group // 16 * 128
        if whole:
            turned = jnp.concatenate([turned[:, -whole:], turned[:, : tokens - whole]], axis=1)
        groups.append(turned[:, :tokens])
    return jnp.concatenate(groups, axis=0)


def attend(queries, key_rows, values, position_bias, counts, donors, first, count, after=()):
    slots, tokens, _ = queries.shape
    vmem = pl.BlockSpec(memory_space=pltpu.VMEM)
    away = pl.BlockSpec(memory_space=pltpu.HBM)
    scores = slots * (CHUNK // HEAD_DIM) * tokens * tokens * count
    return pl.pallas_call(
        functools.partial(attention_kernel, first),
        out_shape=jax.ShapeDtypeStruct((slots * tokens, CHUNK * count), jnp.bfloat16),
        in_specs=[vmem] + [away] * 5 + [pl.BlockSpec(memory_space=pl.ANY)] * len(after),
        out_specs=vmem,
        scratch_shapes=[
            pltpu.VMEM((count, 3, slots, tokens, CHUNK), jnp.bfloat16),
            pltpu.SemaphoreType.DMA((count, 3)),
            pltpu.SMEM(counts.shape, counts.dtype),
            pltpu.SMEM(donors.shape, donors.dtype),
            pltpu.SemaphoreType.DMA((2,)),
        ],
        compiler_params=pltpu.CompilerParams(vmem_limit_bytes=14 << 20),
        cost_estimate=pl.CostEstimate(
            flops=4 * scores * HEAD_DIM,
            bytes_accessed=8 * slots * tokens * CHUNK * count,
            transcendentals=scores,
        ),
    )(position_bias.T, queries, key_rows, values, counts, donors, *after)


def device_index(rep, dp, tensor, dp_size):
    return (rep * dp_size + dp) * 2 + tensor


def ring_order(dp_size):
    half = dp_size // 2
    return [2 * i for i in range(half)] + [2 * i + 1 for i in reversed(range(half))]


def ring_pairs(reps, dp_size, way):
    order = ring_order(dp_size)
    pairs = []
    for rep in range(reps):
        step = way if rep == 0 else -way
        for place in range(dp_size):
            to = order[(place + step) % dp_size]
            for tensor in range(2):
                pairs.append(
                    (
                        device_index(rep, order[place], tensor, dp_size),
                        device_index(rep, to, tensor, dp_size),
                    )
                )
    return pairs


def block_of(distance):
    dp = lax.axis_index("dp")
    place = jnp.where(dp % 2 == 0, dp // 2, 7 - dp // 2)
    way = jnp.where(lax.axis_index("rep") == 0, 1, -1)
    place = (place - way * distance + 16) % 8
    return jnp.where(place < 4, 2 * place, 2 * (7 - place) + 1)


def project_kernel(plan, n_context, n_weights, *refs):
    context = refs[:n_context]
    weights = refs[n_context : n_context + n_weights]
    bases, out_ref = refs[n_context + n_weights : -1], refs[-1]
    for slot, products in enumerate(plan):
        total = bases[0][slot] if bases and slot < bases[0].shape[0] else None
        for source, column, pieces in products:
            parts = [weights[weight][row : row + rows] for weight, row, rows in pieces]
            rows = parts[0] if len(parts) == 1 else jnp.concatenate(parts, axis=0)
            part = jnp.dot(
                context[source][:, column : column + rows.shape[0]],
                rows,
                preferred_element_type=jnp.float32,
            )
            total = part if total is None else total + part
        out_ref[slot] = total.astype(out_ref.dtype)


def project(context, weights, plan, kind, bases=()):
    rows = context[0].shape[0]
    depth = sum(piece[-1] for block in plan for product in block for piece in product[-1])
    vmem = pl.BlockSpec(memory_space=pltpu.VMEM)
    return pl.pallas_call(
        functools.partial(project_kernel, plan, len(context), len(weights)),
        out_shape=jax.ShapeDtypeStruct((len(plan), rows, CHUNK), kind),
        in_specs=[vmem] * (len(context) + len(weights) + len(bases)),
        out_specs=vmem,
        compiler_params=pltpu.CompilerParams(vmem_limit_bytes=12 << 20),
        cost_estimate=pl.CostEstimate(
            flops=2 * rows * depth * CHUNK,
            bytes_accessed=2 * (len(plan) * rows * CHUNK + depth * CHUNK),
            transcendentals=0,
        ),
    )(*context, *weights, *bases)


def finish_kernel(distances, *refs):
    n = len(distances)
    kept, other = refs[:n], refs[n : 2 * n]
    out_ref, buffer, sem = refs[-3:]
    slots, tokens = out_ref.shape[:2]
    tensor = lax.axis_index("tensor")
    steps = []
    for array, group in enumerate(distances):
        for slot, distance in enumerate(group):
            at = len(steps)
            block = block_of(distance)
            column = pl.multiple_of(block % 4 * CHUNK, CHUNK)
            copy = pltpu.make_async_copy(
                buffer.at[at], out_ref.at[:, :, pl.ds(column, CHUNK)], sem.at[at]
            )
            steps.append((block // 4 == tensor, copy))

            @pl.when(block // 4 == tensor)
            def _():
                for passage in range(slots):
                    rows = slice(passage * tokens, (passage + 1) * tokens)
                    buffer[at, passage] = kept[array][slot, rows] + other[array][slot, rows]
                copy.start()

    for mine, copy in steps:

        @pl.when(mine)
        def _():
            copy.wait()


def finish(kept, other, distances, slots, held=()):
    rows = kept[0].shape[1]
    tokens = rows // slots
    vmem = pl.BlockSpec(memory_space=pltpu.VMEM)
    away = pl.BlockSpec(memory_space=pl.ANY)
    blocks = sum(len(group) for group in distances)
    n_in = 2 * len(kept)
    return pl.pallas_call(
        functools.partial(finish_kernel, distances),
        out_shape=jax.ShapeDtypeStruct((slots, tokens, 4 * CHUNK), jnp.bfloat16),
        in_specs=[vmem] * n_in + [away] * len(held),
        out_specs=away,
        scratch_shapes=[
            pltpu.VMEM((blocks, slots, tokens, CHUNK), jnp.bfloat16),
            pltpu.SemaphoreType.DMA((blocks,)),
        ],
        input_output_aliases={n_in: 0} if held else {},
        compiler_params=pltpu.CompilerParams(vmem_limit_bytes=12 << 20),
        cost_estimate=pl.CostEstimate(
            flops=blocks * rows * CHUNK,
            bytes_accessed=blocks * rows * CHUNK * 3,
            transcendentals=0,
        ),
    )(*kept, *other, *held)


def with_ring(queries, key_rows, values, position_bias, out_weight, counts, donors, reps, dp_size):
    slots = queries.shape[0]
    ahead = ring_pairs(reps, dp_size, 1)
    back = ring_pairs(reps, dp_size, -1)
    places = [(r, d, t) for r in range(2) for d in range(dp_size) for t in range(2)]
    across = [
        (device_index(r, d, t, dp_size), device_index(1 - r, d, t, dp_size)) for r, d, t in places
    ]
    cores = [
        (device_index(r, d, t, dp_size), device_index(r, d, 1 - t, dp_size)) for r, d, t in places
    ]
    send = lambda value, pairs: lax.ppermute(value, AXES, pairs)
    depth = out_weight.shape[0]
    half, cut = depth // 2, 11 * depth // 32
    over = half - cut
    lead = over // 128 * 128
    spill = over - lead
    edge = lambda p, q: jnp.concatenate([p[:cut], q[-cut:]], axis=0)
    barrier = lax.optimization_barrier

    p1, q1 = send(out_weight[:-cut], ahead), send(out_weight[cut:], back)
    c0 = attend(queries, key_rows, values, position_bias, counts, donors, 0, 2)
    p1, c0 = barrier((p1, c0))

    p2, q2, y1 = send(p1, ahead), send(q1, back), send(edge(p1, q1), across)
    c1 = attend(queries, key_rows, values, position_bias, counts, donors, 2, 2, (c0,))
    p2, c1 = barrier((p2, c1))
    context = (c0, c1)

    p3, q3, y2 = send(p2, ahead), send(q2, back), send(edge(p2, q2), across)
    p3, q3, y1 = barrier((p3, q3, y1))

    own = [(0, 0, [(0, 0, half)]), (1, 0, [(0, half, half)])]
    p_block = lambda p, y: [(0, 0, [(p, 0, half)]), (1, 0, [(p, half, over), (y, cut, cut)])]
    q_block = lambda q, y: [(0, 0, [(y, 0, cut), (q, 0, over)]), (1, 0, [(q, over, half)])]
    p_part = [(0, 0, [(0, 0, half)]), (1, 0, [(0, half, lead)])]
    q_part = [(0, half - lead, [(1, spill, lead)]), (1, 0, [(1, over, half)])]
    p_rest = [(1, lead, [(0, half + lead, spill), (2, cut, cut)])]
    q_rest = [(0, 0, [(2, 0, cut), (1, 0, spill)])]
    opposite = [(0, 0, [(3, 0, half)]), (1, 0, [(4, 0, half)])]

    p4, q4 = send(p3[:half], ahead), send(q3[-half:], back)
    y3 = send(edge(p3, q3), across)
    e1 = project(
        context, (out_weight, p1, q1, y1), [own, p_block(1, 3), q_block(2, 3)], jnp.bfloat16
    )
    e2 = project(context, (p2, q2, y2), [p_block(0, 2), q_block(1, 2)], jnp.bfloat16)
    started = project(context, (p3, q3), [p_part, q_part], jnp.float32)
    p4, q4, y3, e2, started = barrier((p4, q4, y3, e2, started))

    x1, x2 = send(e1, cores), send(e2, cores)
    e3 = project(
        context, (p3, q3, y3, p4, q4), [p_rest, q_rest, opposite], jnp.bfloat16, (started,)
    )
    x3 = send(e3, cores)
    early = finish((e1, e2), (x1, x2), ((0, 1, -1), (2, -2)), slots)
    x3, early = barrier((x3, early))
    return finish((e3,), (x3,), ((3, -3, 4),), slots, (early,))


def with_gather(queries, key_rows, values, position_bias, out_weight, counts, donors):
    slots, tokens, features = queries.shape
    whole = lax.all_gather(out_weight, "dp", axis=1, tiled=True)
    context = attend(queries, key_rows, values, position_bias, counts, donors, 0, features // CHUNK)
    product = jnp.dot(context, whole, preferred_element_type=jnp.float32).astype(jnp.bfloat16)
    merged = lax.psum_scatter(product, "tensor", scatter_dimension=1, tiled=True)
    return merged.reshape(slots, tokens, merged.shape[1])


def solution(mesh):
    in_specs = (
        P(("rep", "dp"), None, "tensor"),
        P(("rep", "dp"), None, "tensor"),
        P(("rep", "dp"), None, "tensor"),
        P(None, "tensor"),
        P("tensor", "dp"),
        P(("rep", "dp")),
        P("rep"),
    )
    out_specs = P(("rep", "dp"), None, "tensor")
    reps, dp_size = mesh.shape["rep"], mesh.shape["dp"]
    if reps == 2 and dp_size == 8 and mesh.shape["tensor"] == 2:
        on_device = functools.partial(with_ring, reps=reps, dp_size=dp_size)
    else:
        on_device = with_gather
    return jax.shard_map(
        on_device, mesh=mesh, in_specs=in_specs, out_specs=out_specs, check_vma=False
    )
```

```python
import functools

import jax
import jax.numpy as jnp
from jax import lax
from jax.experimental import pallas as pl
from jax.experimental.pallas import tpu as pltpu
from jax.sharding import PartitionSpec as P

HEAD_DIM = 64
PAIR = 2 * HEAD_DIM
CHUNK = 256
THRESHOLDS = (12, 16, 23, 32, 46, 64, 91)
AXES = ("rep", "dp", "tensor")


def bias_rows(position_bias, tokens):
    bucket_count = position_bias.shape[1]
    shape = (bucket_count, 2 * tokens)
    relative = lax.broadcasted_iota(jnp.int32, shape, 1) - (tokens - 1)
    distance = jnp.abs(relative)
    far = jnp.full(shape, 8, jnp.int32)
    for threshold in THRESHOLDS:
        far = far + jnp.where(distance >= threshold, 1, 0)
    bucket = jnp.where(distance < 8, distance, far) + jnp.where(relative > 0, 16, 0)
    one_hot = jnp.where(bucket == lax.broadcasted_iota(jnp.int32, shape, 0), 1.0, 0.0)
    return lax.dot_general(
        position_bias,
        one_hot,
        (((1,), (0,)), ((), ())),
        precision=lax.Precision.HIGHEST,
        preferred_element_type=jnp.float32,
    )


def attention_kernel(first, joined, bias_ref, *refs):
    sources, (out_ref, held, sem) = refs[:3], refs[-3:]
    count, _, slots, tokens, width = held.shape
    offset = out_ref.shape[1] - count * width
    copies = [
        [
            pltpu.make_async_copy(
                source.at[:, :, (first + chunk) * width : (first + chunk + 1) * width],
                held.at[chunk, at],
                sem.at[chunk, at],
            )
            for at, source in enumerate(sources)
        ]
        for chunk in range(count)
    ]
    for chunk in copies:
        for copy in chunk:
            copy.start()
    if joined:
        out_ref[:, :offset] = refs[3][...]
    rows = bias_rows(bias_ref[...], tokens)
    lower = lax.broadcasted_iota(jnp.int32, (tokens, PAIR), 1) < HEAD_DIM
    for chunk in range(count):
        for copy in copies[chunk]:
            copy.wait()
        for pair in range(width // PAIR):
            columns = slice(pair * PAIR, (pair + 1) * PAIR)
            head = (first + chunk) * (width // HEAD_DIM) + 2 * pair
            terms = [toeplitz(rows[head + i : head + i + 1], tokens) for i in range(2)]
            for slot in range(slots):
                query, key, value = (held[chunk, at, slot, :, columns] for at in range(3))
                sums = []
                for i in range(2):
                    own = lower if i == 0 else jnp.logical_not(lower)
                    scores = lax.dot_general(
                        query,
                        jnp.where(own, key, 0),
                        (((1,), (1,)), ((), ())),
                        preferred_element_type=jnp.float32,
                    )
                    scores = scores + terms[i]
                    highest = jnp.max(scores, axis=-1, keepdims=True)
                    expd = jnp.exp(scores - highest).astype(jnp.bfloat16)
                    sums.append(
                        jnp.dot(expd, jnp.where(own, value, 1), preferred_element_type=jnp.float32)
                    )
                weighted = jnp.where(lower, sums[0], sums[1])
                total = pltpu.roll(jnp.where(lower, sums[1], sums[0]), HEAD_DIM, 1)
                at = offset + chunk * width + pair * PAIR
                at = slice(at, at + PAIR)
                out_ref[slot * tokens : (slot + 1) * tokens, at] = (weighted / total).astype(
                    jnp.bfloat16
                )


def toeplitz(row, tokens):
    spread = jnp.broadcast_to(row, (8, 2 * tokens))
    base = pltpu.roll(spread, tokens + 1, 1, stride=1, stride_axis=0)
    rolled = [base if i == 0 else pltpu.roll(base, 8 * i, 1) for i in range(16)]
    groups = []
    for group in range(tokens // 8):
        turned, whole = rolled[group % 16], group // 16 * 128
        if whole:
            turned = jnp.concatenate([turned[:, -whole:], turned[:, : tokens - whole]], axis=1)
        groups.append(turned[:, :tokens])
    return jnp.concatenate(groups, axis=0)


def attend(queries, key_rows, values, position_bias, first, count, after=(), joined=False):
    slots, tokens, _ = queries.shape
    vmem = pl.BlockSpec(memory_space=pltpu.VMEM)
    away = pl.BlockSpec(memory_space=pltpu.HBM)
    last = vmem if joined else pl.BlockSpec(memory_space=pl.ANY)
    columns = CHUNK * count + (after[0].shape[1] if joined else 0)
    scores = slots * (CHUNK // HEAD_DIM) * tokens * tokens * count
    return pl.pallas_call(
        functools.partial(attention_kernel, first, joined),
        out_shape=jax.ShapeDtypeStruct((slots * tokens, columns), jnp.bfloat16),
        in_specs=[vmem] + [away] * 3 + [last] * len(after),
        out_specs=vmem,
        scratch_shapes=[
            pltpu.VMEM((count, 3, slots, tokens, CHUNK), jnp.bfloat16),
            pltpu.SemaphoreType.DMA((count, 3)),
        ],
        compiler_params=pltpu.CompilerParams(vmem_limit_bytes=14 << 20),
        cost_estimate=pl.CostEstimate(
            flops=4 * scores * HEAD_DIM,
            bytes_accessed=8 * slots * tokens * CHUNK * count,
            transcendentals=scores,
        ),
    )(position_bias.T, queries, key_rows, values, *after)


def device_index(rep, dp, tensor, dp_size):
    return (rep * dp_size + dp) * 2 + tensor


def ring_order(dp_size):
    half = dp_size // 2
    return [2 * i for i in range(half)] + [2 * i + 1 for i in reversed(range(half))]


def ring_pairs(reps, dp_size, way):
    order = ring_order(dp_size)
    pairs = []
    for rep in range(reps):
        step = way if rep == 0 else -way
        for place in range(dp_size):
            to = order[(place + step) % dp_size]
            for tensor in range(2):
                pairs.append(
                    (
                        device_index(rep, order[place], tensor, dp_size),
                        device_index(rep, to, tensor, dp_size),
                    )
                )
    return pairs


def block_of(distance):
    dp = lax.axis_index("dp")
    place = jnp.where(dp % 2 == 0, dp // 2, 7 - dp // 2)
    way = jnp.where(lax.axis_index("rep") == 0, 1, -1)
    place = (place - way * distance + 16) % 8
    return jnp.where(place < 4, 2 * place, 2 * (7 - place) + 1)


def project_kernel(plan, n_context, n_weights, choice, *refs):
    context = refs[:n_context]
    weights = refs[n_context : n_context + n_weights]
    n_out = 2 if choice else 1
    bases, out_ref = refs[n_context + n_weights : -n_out], refs[-n_out]
    for slot, products in enumerate(plan):
        total = bases[0][slot] if bases and slot < bases[0].shape[0] else None
        for source, column, pieces in products:
            parts = [weights[weight][row : row + rows] for weight, row, rows in pieces]
            rows = parts[0] if len(parts) == 1 else jnp.concatenate(parts, axis=0)
            part = jnp.dot(
                context[source][:, column : column + rows.shape[0]],
                rows,
                preferred_element_type=jnp.float32,
            )
            total = part if total is None else total + part
        out_ref[slot] = total.astype(out_ref.dtype)
        if choice:

            @pl.when(block_of(choice[slot]) // 4 != lax.axis_index("tensor"))
            def _():
                refs[-1][0] = total.astype(out_ref.dtype)


def project(context, weights, plan, kind, bases=(), choice=None):
    rows = context[0].shape[0]
    depth = sum(piece[-1] for block in plan for product in block for piece in product[-1])
    vmem = pl.BlockSpec(memory_space=pltpu.VMEM)
    return pl.pallas_call(
        functools.partial(project_kernel, plan, len(context), len(weights), choice),
        out_shape=[
            jax.ShapeDtypeStruct((blocks, rows, CHUNK), kind)
            for blocks in ((len(plan), 1) if choice else (len(plan),))
        ],
        in_specs=[vmem] * (len(context) + len(weights) + len(bases)),
        out_specs=[vmem] * (2 if choice else 1),
        compiler_params=pltpu.CompilerParams(vmem_limit_bytes=12 << 20),
        cost_estimate=pl.CostEstimate(
            flops=2 * rows * depth * CHUNK,
            bytes_accessed=2 * (len(plan) * rows * CHUNK + depth * CHUNK),
            transcendentals=0,
        ),
    )(*context, *weights, *bases)


def finish_kernel(distances, counts_ref, donors_ref, *refs):
    n = len(distances)
    kept, other = refs[:n], refs[n : 2 * n]
    out_ref, buffer, sem = refs[-3:]
    slots, tokens = out_ref.shape[:2]
    my_group, tensor = lax.axis_index("dp"), lax.axis_index("tensor")
    second = donors_ref[0] == my_group
    for at in range(1, donors_ref.shape[0]):
        second = jnp.logical_or(second, donors_ref[at] == my_group)
    live = [
        jnp.where(lives, 1.0, 0.0).astype(jnp.bfloat16) for lives in (counts_ref[0] >= 1, second)
    ]
    at = 0
    steps = []
    for array, group in enumerate(distances):
        several = other[array].shape[0] > 1
        for slot, distance in enumerate(group):
            block = block_of(distance)
            column = pl.multiple_of(block % 4 * CHUNK, CHUNK)
            copy = pltpu.make_async_copy(
                buffer.at[at], out_ref.at[:, :, pl.ds(column, CHUNK)], sem.at[at]
            )
            steps.append((block // 4 == tensor, copy))

            @pl.when(block // 4 == tensor)
            def _():
                for passage in range(slots):
                    rows = slice(passage * tokens, (passage + 1) * tokens)
                    both = kept[array][slot, rows] + other[array][slot if several else 0, rows]
                    buffer[at, passage] = both * live[passage]
                copy.start()

            at += 1
    for mine, copy in steps:

        @pl.when(mine)
        def _():
            copy.wait()


def finish(kept, other, distances, counts, donors, slots, held=()):
    rows = kept[0].shape[1]
    tokens = rows // slots
    smem = pl.BlockSpec(memory_space=pltpu.SMEM)
    vmem = pl.BlockSpec(memory_space=pltpu.VMEM)
    away = pl.BlockSpec(memory_space=pl.ANY)
    blocks = sum(len(group) for group in distances)
    n_in = 2 + 2 * len(kept)
    return pl.pallas_call(
        functools.partial(finish_kernel, distances),
        out_shape=jax.ShapeDtypeStruct((slots, tokens, 4 * CHUNK), jnp.bfloat16),
        in_specs=[smem, smem] + [vmem] * (n_in - 2) + [away] * len(held),
        out_specs=away,
        scratch_shapes=[
            pltpu.VMEM((blocks, slots, tokens, CHUNK), jnp.bfloat16),
            pltpu.SemaphoreType.DMA((blocks,)),
        ],
        input_output_aliases={n_in: 0} if held else {},
        compiler_params=pltpu.CompilerParams(vmem_limit_bytes=12 << 20),
        cost_estimate=pl.CostEstimate(
            flops=blocks * rows * CHUNK,
            bytes_accessed=blocks * rows * CHUNK * 3,
            transcendentals=0,
        ),
    )(counts, donors, *kept, *other, *held)


def with_ring(queries, key_rows, values, position_bias, out_weight, counts, donors, reps, dp_size):
    slots = queries.shape[0]
    ahead = ring_pairs(reps, dp_size, 1)
    back = ring_pairs(reps, dp_size, -1)
    places = [(r, d, t) for r in range(2) for d in range(dp_size) for t in range(2)]
    across = [
        (device_index(r, d, t, dp_size), device_index(1 - r, d, t, dp_size)) for r, d, t in places
    ]
    cores = [
        (device_index(r, d, t, dp_size), device_index(r, d, 1 - t, dp_size)) for r, d, t in places
    ]
    send = lambda value, pairs: lax.ppermute(value, AXES, pairs)
    depth = out_weight.shape[0]
    half, cut = depth // 2, 11 * depth // 32
    over = half - cut
    lead = over // 128 * 128
    spill = over - lead
    edge = lambda p, q: jnp.concatenate([p[:cut], q[-cut:]], axis=0)
    barrier = lax.optimization_barrier

    p1, q1 = send(out_weight[:-cut], ahead), send(out_weight[cut:], back)
    c0 = attend(queries, key_rows, values, position_bias, 0, 2)
    p1, c0 = barrier((p1, c0))

    p2, q2, y1 = send(p1, ahead), send(q1, back), send(edge(p1, q1), across)
    c1 = attend(queries, key_rows, values, position_bias, 2, 1, (c0,))
    p2, c1 = barrier((p2, c1))

    p3, q3, y2 = send(p2, ahead), send(q2, back), send(edge(p2, q2), across)
    c1 = attend(queries, key_rows, values, position_bias, 3, 1, (c1,), joined=True)
    p3, q3, y1, c1 = barrier((p3, q3, y1, c1))
    context = (c0, c1)

    own = [(0, 0, [(0, 0, half)]), (1, 0, [(0, half, half)])]
    p_block = lambda p, y: [(0, 0, [(p, 0, half)]), (1, 0, [(p, half, over), (y, cut, cut)])]
    q_block = lambda q, y: [(0, 0, [(y, 0, cut), (q, 0, over)]), (1, 0, [(q, over, half)])]
    p_part = [(0, 0, [(0, 0, half)]), (1, 0, [(0, half, lead)])]
    q_part = [(0, half - lead, [(1, spill, lead)]), (1, 0, [(1, over, half)])]
    p_rest = [(1, lead, [(0, half + lead, spill), (2, cut, cut)])]
    q_rest = [(0, 0, [(2, 0, cut), (1, 0, spill)])]
    opposite = [(0, 0, [(3, 0, half)]), (1, 0, [(4, 0, half)])]

    p4, q4 = send(p3[:half], ahead), send(q3[-half:], back)
    y3 = send(edge(p3, q3), across)
    (e1,) = project(
        context, (out_weight, p1, q1, y1), [own, p_block(1, 3), q_block(2, 3)], jnp.bfloat16
    )
    e2, s2 = project(
        context, (p2, q2, y2), [p_block(0, 2), q_block(1, 2)], jnp.bfloat16, choice=(2, -2)
    )
    (started,) = project(context, (p3, q3), [p_part, q_part], jnp.float32)
    p4, q4, y3, e2, s2, started = barrier((p4, q4, y3, e2, s2, started))

    x1, x2 = send(e1, cores), send(s2, cores)
    (e3,) = project(
        context, (p3, q3, y3, p4, q4), [p_rest, q_rest, opposite], jnp.bfloat16, (started,)
    )
    x3 = send(e3, cores)
    early = finish((e1,), (x1,), ((0, 1, -1),), counts, donors, slots)
    x2, x3, early = barrier((x2, x3, early))
    return finish((e2, e3), (x2, x3), ((2, -2), (3, -3, 4)), counts, donors, slots, (early,))


def with_gather(queries, key_rows, values, position_bias, out_weight, counts, donors):
    slots, tokens, features = queries.shape
    whole = lax.all_gather(out_weight, "dp", axis=1, tiled=True)
    context = attend(queries, key_rows, values, position_bias, 0, features // CHUNK)
    product = jnp.dot(context, whole, preferred_element_type=jnp.float32).astype(jnp.bfloat16)
    merged = lax.psum_scatter(product, "tensor", scatter_dimension=1, tiled=True)
    first_live = counts[0] >= 1
    second_live = jnp.any(donors == lax.axis_index("dp"))
    live = jnp.stack([first_live, second_live]).astype(jnp.bfloat16)
    return merged.reshape(slots, tokens, merged.shape[1]) * live[:, None, None]


def solution(mesh):
    in_specs = (
        P(("rep", "dp"), None, "tensor"),
        P(("rep", "dp"), None, "tensor"),
        P(("rep", "dp"), None, "tensor"),
        P(None, "tensor"),
        P("tensor", "dp"),
        P(("rep", "dp")),
        P("rep"),
    )
    out_specs = P(("rep", "dp"), None, "tensor")
    reps, dp_size = mesh.shape["rep"], mesh.shape["dp"]
    if reps == 2 and dp_size == 8 and mesh.shape["tensor"] == 2:
        on_device = functools.partial(with_ring, reps=reps, dp_size=dp_size)
    else:
        on_device = with_gather
    return jax.shard_map(
        on_device, mesh=mesh, in_specs=in_specs, out_specs=out_specs, check_vma=False
    )
```

```python
import functools

import jax
import jax.numpy as jnp
from jax import lax
from jax.experimental import pallas as pl
from jax.experimental.pallas import tpu as pltpu
from jax.sharding import PartitionSpec as P

HEAD_DIM = 64
PAIR = 2 * HEAD_DIM
CHUNK = 256
LIVE_ROWS = 16
THRESHOLDS = (12, 16, 23, 32, 46, 64, 91)
AXES = ("rep", "dp", "tensor")


def bias_rows(position_bias, tokens):
    bucket_count = position_bias.shape[1]
    shape = (bucket_count, 2 * tokens)
    relative = lax.broadcasted_iota(jnp.int32, shape, 1) - (tokens - 1)
    distance = jnp.abs(relative)
    far = jnp.full(shape, 8, jnp.int32)
    for threshold in THRESHOLDS:
        far = far + jnp.where(distance >= threshold, 1, 0)
    bucket = jnp.where(distance < 8, distance, far) + jnp.where(relative > 0, 16, 0)
    one_hot = jnp.where(bucket == lax.broadcasted_iota(jnp.int32, shape, 0), 1.0, 0.0)
    return lax.dot_general(
        position_bias,
        one_hot,
        (((1,), (0,)), ((), ())),
        precision=lax.Precision.HIGHEST,
        preferred_element_type=jnp.float32,
    )


def attention_kernel(first, joined, bias_ref, *refs):
    sources, (out_ref, held, sem) = refs[:3], refs[-3:]
    count, _, slots, tokens, width = held.shape
    offset = out_ref.shape[1] - count * width
    copies = [
        [
            pltpu.make_async_copy(
                source.at[:, :, (first + chunk) * width : (first + chunk + 1) * width],
                held.at[chunk, at],
                sem.at[chunk, at],
            )
            for at, source in enumerate(sources)
        ]
        for chunk in range(count)
    ]
    for chunk in copies:
        for copy in chunk:
            copy.start()
    if joined:
        out_ref[:, :offset] = refs[3][...]
    rows = bias_rows(bias_ref[...], tokens)
    lower = lax.broadcasted_iota(jnp.int32, (tokens, PAIR), 1) < HEAD_DIM
    for chunk in range(count):
        for copy in copies[chunk]:
            copy.wait()
        for pair in range(width // PAIR):
            columns = slice(pair * PAIR, (pair + 1) * PAIR)
            head = (first + chunk) * (width // HEAD_DIM) + 2 * pair
            terms = [toeplitz(rows[head + i : head + i + 1], tokens) for i in range(2)]
            for slot in range(slots):
                query, key, value = (held[chunk, at, slot, :, columns] for at in range(3))
                sums = []
                for i in range(2):
                    own = lower if i == 0 else jnp.logical_not(lower)
                    scores = lax.dot_general(
                        query,
                        jnp.where(own, key, 0),
                        (((1,), (1,)), ((), ())),
                        preferred_element_type=jnp.float32,
                    )
                    scores = scores + terms[i]
                    highest = jnp.max(scores, axis=-1, keepdims=True)
                    expd = jnp.exp(scores - highest).astype(jnp.bfloat16)
                    sums.append(
                        jnp.dot(expd, jnp.where(own, value, 1), preferred_element_type=jnp.float32)
                    )
                weighted = jnp.where(lower, sums[0], sums[1])
                total = pltpu.roll(jnp.where(lower, sums[1], sums[0]), HEAD_DIM, 1)
                at = offset + chunk * width + pair * PAIR
                at = slice(at, at + PAIR)
                out_ref[slot * tokens : (slot + 1) * tokens, at] = (weighted / total).astype(
                    jnp.bfloat16
                )


def toeplitz(row, tokens):
    spread = jnp.broadcast_to(row, (8, 2 * tokens))
    base = pltpu.roll(spread, tokens + 1, 1, stride=1, stride_axis=0)
    rolled = [base if i == 0 else pltpu.roll(base, 8 * i, 1) for i in range(16)]
    groups = []
    for group in range(tokens // 8):
        turned, whole = rolled[group % 16], group // 16 * 128
        if whole:
            turned = jnp.concatenate([turned[:, -whole:], turned[:, : tokens - whole]], axis=1)
        groups.append(turned[:, :tokens])
    return jnp.concatenate(groups, axis=0)


def attend(queries, key_rows, values, position_bias, first, count, after=(), joined=False):
    slots, tokens, _ = queries.shape
    vmem = pl.BlockSpec(memory_space=pltpu.VMEM)
    away = pl.BlockSpec(memory_space=pltpu.HBM)
    last = vmem if joined else pl.BlockSpec(memory_space=pl.ANY)
    columns = CHUNK * count + (after[0].shape[1] if joined else 0)
    scores = slots * (CHUNK // HEAD_DIM) * tokens * tokens * count
    return pl.pallas_call(
        functools.partial(attention_kernel, first, joined),
        out_shape=jax.ShapeDtypeStruct((slots * tokens, columns), jnp.bfloat16),
        in_specs=[vmem] + [away] * 3 + [last] * len(after),
        out_specs=vmem,
        scratch_shapes=[
            pltpu.VMEM((count, 3, slots, tokens, CHUNK), jnp.bfloat16),
            pltpu.SemaphoreType.DMA((count, 3)),
        ],
        compiler_params=pltpu.CompilerParams(vmem_limit_bytes=14 << 20),
        cost_estimate=pl.CostEstimate(
            flops=4 * scores * HEAD_DIM,
            bytes_accessed=8 * slots * tokens * CHUNK * count,
            transcendentals=scores,
        ),
    )(position_bias.T, queries, key_rows, values, *after)


def device_index(rep, dp, tensor, dp_size):
    return (rep * dp_size + dp) * 2 + tensor


def ring_order(dp_size):
    half = dp_size // 2
    return [2 * i for i in range(half)] + [2 * i + 1 for i in reversed(range(half))]


def ring_pairs(reps, dp_size, way):
    order = ring_order(dp_size)
    pairs = []
    for rep in range(reps):
        step = way if rep == 0 else -way
        for place in range(dp_size):
            to = order[(place + step) % dp_size]
            for tensor in range(2):
                pairs.append(
                    (
                        device_index(rep, order[place], tensor, dp_size),
                        device_index(rep, to, tensor, dp_size),
                    )
                )
    return pairs


def block_of(distance):
    dp = lax.axis_index("dp")
    place = jnp.where(dp % 2 == 0, dp // 2, 7 - dp // 2)
    way = jnp.where(lax.axis_index("rep") == 0, 1, -1)
    place = (place - way * distance + 16) % 8
    return jnp.where(place < 4, 2 * place, 2 * (7 - place) + 1)


def project_kernel(plan, n_context, n_weights, choice, *refs):
    context = refs[:n_context]
    weights = refs[n_context : n_context + n_weights]
    n_out = 2 if choice else 1
    bases, out_ref = refs[n_context + n_weights : -n_out], refs[-n_out]
    for slot, products in enumerate(plan):
        total = bases[0][slot] if bases and slot < bases[0].shape[0] else None
        for source, column, pieces in products:
            parts = [weights[weight][row : row + rows] for weight, row, rows in pieces]
            rows = parts[0] if len(parts) == 1 else jnp.concatenate(parts, axis=0)
            part = jnp.dot(
                context[source][:, column : column + rows.shape[0]],
                rows,
                preferred_element_type=jnp.float32,
            )
            total = part if total is None else total + part
        out_ref[slot] = total.astype(out_ref.dtype)
        if choice:

            @pl.when(block_of(choice[slot]) // 4 != lax.axis_index("tensor"))
            def _():
                refs[-1][0] = total.astype(out_ref.dtype)


def project(context, weights, plan, kind, bases=(), choice=None):
    rows = context[0].shape[0]
    depth = sum(piece[-1] for block in plan for product in block for piece in product[-1])
    vmem = pl.BlockSpec(memory_space=pltpu.VMEM)
    return pl.pallas_call(
        functools.partial(project_kernel, plan, len(context), len(weights), choice),
        out_shape=[
            jax.ShapeDtypeStruct((blocks, rows, CHUNK), kind)
            for blocks in ((len(plan), 1) if choice else (len(plan),))
        ],
        in_specs=[vmem] * (len(context) + len(weights) + len(bases)),
        out_specs=[vmem] * (2 if choice else 1),
        compiler_params=pltpu.CompilerParams(vmem_limit_bytes=12 << 20),
        cost_estimate=pl.CostEstimate(
            flops=2 * rows * depth * CHUNK,
            bytes_accessed=2 * (len(plan) * rows * CHUNK + depth * CHUNK),
            transcendentals=0,
        ),
    )(*context, *weights, *bases)


def live_kernel(counts_ref, donors_ref, after_ref, out_ref):
    my_group = lax.axis_index("dp")
    second = donors_ref[0] == my_group
    for at in range(1, donors_ref.shape[0]):
        second = jnp.logical_or(second, donors_ref[at] == my_group)
    for slot, lives in enumerate((counts_ref[0] >= 1, second)):
        rows = jnp.full((LIVE_ROWS, CHUNK), jnp.where(lives, 1.0, 0.0), jnp.float32)
        out_ref[slot * LIVE_ROWS : (slot + 1) * LIVE_ROWS] = rows.astype(jnp.bfloat16)


def live_slots(counts, donors, after):
    smem = pl.BlockSpec(memory_space=pltpu.SMEM)
    return pl.pallas_call(
        live_kernel,
        out_shape=jax.ShapeDtypeStruct((2 * LIVE_ROWS, CHUNK), jnp.bfloat16),
        in_specs=[smem, smem, pl.BlockSpec(memory_space=pl.ANY)],
        out_specs=pl.BlockSpec(memory_space=pltpu.VMEM),
        compiler_params=pltpu.CompilerParams(vmem_limit_bytes=4 << 20),
    )(counts, donors, after)


def finish_kernel(distances, live_ref, *refs):
    n = len(distances)
    kept, other = refs[:n], refs[n : 2 * n]
    out_ref, buffer, sem = refs[-3:]
    slots, tokens = out_ref.shape[:2]
    tensor = lax.axis_index("tensor")
    steps = []
    for array, group in enumerate(distances):
        several = other[array].shape[0] > 1
        for slot, distance in enumerate(group):
            at = len(steps)
            block = block_of(distance)
            column = pl.multiple_of(block % 4 * CHUNK, CHUNK)
            copies = [
                pltpu.make_async_copy(
                    buffer.at[at, passage],
                    out_ref.at[passage, :, pl.ds(column, CHUNK)],
                    sem.at[at, passage],
                )
                for passage in range(slots)
            ]
            steps.append((block // 4 == tensor, copies))

            @pl.when(block // 4 == tensor)
            def _():
                for passage in range(slots):
                    rows = slice(passage * tokens, (passage + 1) * tokens)
                    both = kept[array][slot, rows] + other[array][slot if several else 0, rows]
                    live = live_ref[passage * LIVE_ROWS : passage * LIVE_ROWS + 1]
                    buffer[at, passage] = both * jnp.broadcast_to(live, both.shape)
                    copies[passage].start()

    for mine, copies in steps:

        @pl.when(mine)
        def _():
            for copy in copies:
                copy.wait()


def finish(kept, other, distances, live, slots, held=()):
    rows = kept[0].shape[1]
    tokens = rows // slots
    vmem = pl.BlockSpec(memory_space=pltpu.VMEM)
    away = pl.BlockSpec(memory_space=pl.ANY)
    blocks = sum(len(group) for group in distances)
    n_in = 1 + 2 * len(kept)
    return pl.pallas_call(
        functools.partial(finish_kernel, distances),
        out_shape=jax.ShapeDtypeStruct((slots, tokens, 4 * CHUNK), jnp.bfloat16),
        in_specs=[vmem] * n_in + [away] * len(held),
        out_specs=away,
        scratch_shapes=[
            pltpu.VMEM((blocks, slots, tokens, CHUNK), jnp.bfloat16),
            pltpu.SemaphoreType.DMA((blocks, slots)),
        ],
        input_output_aliases={n_in: 0} if held else {},
        compiler_params=pltpu.CompilerParams(vmem_limit_bytes=12 << 20),
        cost_estimate=pl.CostEstimate(
            flops=blocks * rows * CHUNK,
            bytes_accessed=blocks * rows * CHUNK * 3,
            transcendentals=0,
        ),
    )(live, *kept, *other, *held)


def with_ring(queries, key_rows, values, position_bias, out_weight, counts, donors, reps, dp_size):
    slots = queries.shape[0]
    ahead = ring_pairs(reps, dp_size, 1)
    back = ring_pairs(reps, dp_size, -1)
    places = [(r, d, t) for r in range(2) for d in range(dp_size) for t in range(2)]
    across = [
        (device_index(r, d, t, dp_size), device_index(1 - r, d, t, dp_size)) for r, d, t in places
    ]
    cores = [
        (device_index(r, d, t, dp_size), device_index(r, d, 1 - t, dp_size)) for r, d, t in places
    ]
    send = lambda value, pairs: lax.ppermute(value, AXES, pairs)
    depth = out_weight.shape[0]
    half, cut = depth // 2, 11 * depth // 32
    over = half - cut
    lead = over // 128 * 128
    spill = over - lead
    edge = lambda p, q: jnp.concatenate([p[:cut], q[-cut:]], axis=0)
    barrier = lax.optimization_barrier

    p1, q1 = send(out_weight[:-cut], ahead), send(out_weight[cut:], back)
    c0 = attend(queries, key_rows, values, position_bias, 0, 2)
    p1, c0 = barrier((p1, c0))

    p2, q2, y1 = send(p1, ahead), send(q1, back), send(edge(p1, q1), across)
    c1 = attend(queries, key_rows, values, position_bias, 2, 1, (c0,))
    live = live_slots(counts, donors, c0)
    p2, c1, live = barrier((p2, c1, live))

    p3, q3, y2 = send(p2, ahead), send(q2, back), send(edge(p2, q2), across)
    c1 = attend(queries, key_rows, values, position_bias, 3, 1, (c1,), joined=True)
    p3, q3, y1, c1 = barrier((p3, q3, y1, c1))
    context = (c0, c1)

    own = [(0, 0, [(0, 0, half)]), (1, 0, [(0, half, half)])]
    p_block = lambda p, y: [(0, 0, [(p, 0, half)]), (1, 0, [(p, half, over), (y, cut, cut)])]
    q_block = lambda q, y: [(0, 0, [(y, 0, cut), (q, 0, over)]), (1, 0, [(q, over, half)])]
    p_part = [(0, 0, [(0, 0, half)]), (1, 0, [(0, half, lead)])]
    q_part = [(0, half - lead, [(1, spill, lead)]), (1, 0, [(1, over, half)])]
    p_rest = [(1, lead, [(0, half + lead, spill), (2, cut, cut)])]
    q_rest = [(0, 0, [(2, 0, cut), (1, 0, spill)])]
    opposite = [(0, 0, [(3, 0, half)]), (1, 0, [(4, 0, half)])]

    p4, q4 = send(p3[:half], ahead), send(q3[-half:], back)
    y3 = send(edge(p3, q3), across)
    (e1,) = project(
        context, (out_weight, p1, q1, y1), [own, p_block(1, 3), q_block(2, 3)], jnp.bfloat16
    )
    e2, s2 = project(
        context, (p2, q2, y2), [p_block(0, 2), q_block(1, 2)], jnp.bfloat16, choice=(2, -2)
    )
    (started,) = project(context, (p3, q3), [p_part, q_part], jnp.float32)
    p4, q4, y3, e2, s2, started = barrier((p4, q4, y3, e2, s2, started))

    x1, x2 = send(e1, cores), send(s2, cores)
    (e3,) = project(
        context, (p3, q3, y3, p4, q4), [p_rest, q_rest, opposite], jnp.bfloat16, (started,)
    )
    x3 = send(e3, cores)
    early = finish((e1,), (x1,), ((0, 1, -1),), live, slots)
    x2, x3, early = barrier((x2, x3, early))
    return finish((e2, e3), (x2, x3), ((2, -2), (3, -3, 4)), live, slots, (early,))


def with_gather(queries, key_rows, values, position_bias, out_weight, counts, donors):
    slots, tokens, features = queries.shape
    whole = lax.all_gather(out_weight, "dp", axis=1, tiled=True)
    context = attend(queries, key_rows, values, position_bias, 0, features // CHUNK)
    product = jnp.dot(context, whole, preferred_element_type=jnp.float32).astype(jnp.bfloat16)
    merged = lax.psum_scatter(product, "tensor", scatter_dimension=1, tiled=True)
    first_live = counts[0] >= 1
    second_live = jnp.any(donors == lax.axis_index("dp"))
    live = jnp.stack([first_live, second_live]).astype(jnp.bfloat16)
    return merged.reshape(slots, tokens, merged.shape[1]) * live[:, None, None]


def solution(mesh):
    in_specs = (
        P(("rep", "dp"), None, "tensor"),
        P(("rep", "dp"), None, "tensor"),
        P(("rep", "dp"), None, "tensor"),
        P(None, "tensor"),
        P("tensor", "dp"),
        P(("rep", "dp")),
        P("rep"),
    )
    out_specs = P(("rep", "dp"), None, "tensor")
    reps, dp_size = mesh.shape["rep"], mesh.shape["dp"]
    if reps == 2 and dp_size == 8 and mesh.shape["tensor"] == 2:
        on_device = functools.partial(with_ring, reps=reps, dp_size=dp_size)
    else:
        on_device = with_gather
    return jax.shard_map(
        on_device, mesh=mesh, in_specs=in_specs, out_specs=out_specs, check_vma=False
    )
```

```python
import functools

import jax
import jax.numpy as jnp
from jax import lax
from jax.experimental import pallas as pl
from jax.experimental.pallas import tpu as pltpu
from jax.sharding import PartitionSpec as P

HEAD_DIM = 64
PAIR = 2 * HEAD_DIM
CHUNK = 256
LIVE_ROWS = 16
THRESHOLDS = (12, 16, 23, 32, 46, 64, 91)
AXES = ("rep", "dp", "tensor")


def bias_rows(position_bias, tokens):
    bucket_count = position_bias.shape[1]
    shape = (bucket_count, 2 * tokens)
    relative = lax.broadcasted_iota(jnp.int32, shape, 1) - (tokens - 1)
    distance = jnp.abs(relative)
    far = jnp.full(shape, 8, jnp.int32)
    for threshold in THRESHOLDS:
        far = far + jnp.where(distance >= threshold, 1, 0)
    bucket = jnp.where(distance < 8, distance, far) + jnp.where(relative > 0, 16, 0)
    one_hot = jnp.where(bucket == lax.broadcasted_iota(jnp.int32, shape, 0), 1.0, 0.0)
    return lax.dot_general(
        position_bias,
        one_hot,
        (((1,), (0,)), ((), ())),
        precision=lax.Precision.HIGHEST,
        preferred_element_type=jnp.float32,
    )


def attention_kernel(first, joined, bias_ref, *refs):
    sources, (out_ref, held, sem) = refs[:3], refs[-3:]
    count, _, slots, tokens, width = held.shape
    offset = out_ref.shape[1] - count * width
    copies = [
        [
            pltpu.make_async_copy(
                source.at[:, :, (first + chunk) * width : (first + chunk + 1) * width],
                held.at[chunk, at],
                sem.at[chunk, at],
            )
            for at, source in enumerate(sources)
        ]
        for chunk in range(count)
    ]
    for chunk in copies:
        for copy in chunk:
            copy.start()
    if joined:
        out_ref[:, :offset] = refs[3][...]
    rows = bias_rows(bias_ref[...], tokens)
    lower = lax.broadcasted_iota(jnp.int32, (tokens, PAIR), 1) < HEAD_DIM
    for chunk in range(count):
        for copy in copies[chunk]:
            copy.wait()
        for pair in range(width // PAIR):
            columns = slice(pair * PAIR, (pair + 1) * PAIR)
            head = (first + chunk) * (width // HEAD_DIM) + 2 * pair
            terms = [toeplitz(rows[head + i : head + i + 1], tokens) for i in range(2)]
            for slot in range(slots):
                query, key, value = (held[chunk, at, slot, :, columns] for at in range(3))
                sums = []
                for i in range(2):
                    own = lower if i == 0 else jnp.logical_not(lower)
                    scores = lax.dot_general(
                        query,
                        jnp.where(own, key, 0),
                        (((1,), (1,)), ((), ())),
                        preferred_element_type=jnp.float32,
                    )
                    scores = scores + terms[i]
                    highest = jnp.max(scores, axis=-1, keepdims=True)
                    expd = jnp.exp(scores - highest).astype(jnp.bfloat16)
                    sums.append(
                        jnp.dot(expd, jnp.where(own, value, 1), preferred_element_type=jnp.float32)
                    )
                weighted = jnp.where(lower, sums[0], sums[1])
                total = pltpu.roll(jnp.where(lower, sums[1], sums[0]), HEAD_DIM, 1)
                at = offset + chunk * width + pair * PAIR
                at = slice(at, at + PAIR)
                out_ref[slot * tokens : (slot + 1) * tokens, at] = (weighted / total).astype(
                    jnp.bfloat16
                )


def toeplitz(row, tokens):
    spread = jnp.broadcast_to(row, (8, 2 * tokens))
    base = pltpu.roll(spread, tokens + 1, 1, stride=1, stride_axis=0)
    rolled = [base if i == 0 else pltpu.roll(base, 8 * i, 1) for i in range(16)]
    groups = []
    for group in range(tokens // 8):
        turned, whole = rolled[group % 16], group // 16 * 128
        if whole:
            turned = jnp.concatenate([turned[:, -whole:], turned[:, : tokens - whole]], axis=1)
        groups.append(turned[:, :tokens])
    return jnp.concatenate(groups, axis=0)


def attend(queries, key_rows, values, position_bias, first, count, after=(), joined=False):
    slots, tokens, _ = queries.shape
    vmem = pl.BlockSpec(memory_space=pltpu.VMEM)
    away = pl.BlockSpec(memory_space=pltpu.HBM)
    last = vmem if joined else pl.BlockSpec(memory_space=pl.ANY)
    columns = CHUNK * count + (after[0].shape[1] if joined else 0)
    scores = slots * (CHUNK // HEAD_DIM) * tokens * tokens * count
    return pl.pallas_call(
        functools.partial(attention_kernel, first, joined),
        out_shape=jax.ShapeDtypeStruct((slots * tokens, columns), jnp.bfloat16),
        in_specs=[vmem] + [away] * 3 + [last] * len(after),
        out_specs=vmem,
        scratch_shapes=[
            pltpu.VMEM((count, 3, slots, tokens, CHUNK), jnp.bfloat16),
            pltpu.SemaphoreType.DMA((count, 3)),
        ],
        compiler_params=pltpu.CompilerParams(vmem_limit_bytes=14 << 20),
        cost_estimate=pl.CostEstimate(
            flops=4 * scores * HEAD_DIM,
            bytes_accessed=8 * slots * tokens * CHUNK * count,
            transcendentals=scores,
        ),
    )(position_bias.T, queries, key_rows, values, *after)


def device_index(rep, dp, tensor, dp_size):
    return (rep * dp_size + dp) * 2 + tensor


def ring_order(dp_size):
    half = dp_size // 2
    return [2 * i for i in range(half)] + [2 * i + 1 for i in reversed(range(half))]


def ring_pairs(reps, dp_size, way):
    order = ring_order(dp_size)
    pairs = []
    for rep in range(reps):
        step = way if rep == 0 else -way
        for place in range(dp_size):
            to = order[(place + step) % dp_size]
            for tensor in range(2):
                pairs.append(
                    (
                        device_index(rep, order[place], tensor, dp_size),
                        device_index(rep, to, tensor, dp_size),
                    )
                )
    return pairs


def block_of(distance):
    dp = lax.axis_index("dp")
    place = jnp.where(dp % 2 == 0, dp // 2, 7 - dp // 2)
    way = jnp.where(lax.axis_index("rep") == 0, 1, -1)
    place = (place - way * distance + 16) % 8
    return jnp.where(place < 4, 2 * place, 2 * (7 - place) + 1)


def project_kernel(plan, n_context, n_weights, choice, *refs):
    context = refs[:n_context]
    weights = refs[n_context : n_context + n_weights]
    n_out = 2 if choice else 1
    bases, out_ref = refs[n_context + n_weights : -n_out], refs[-n_out]
    for slot, products in enumerate(plan):
        total = bases[0][slot] if bases and slot < bases[0].shape[0] else None
        for source, column, pieces in products:
            parts = [weights[weight][row : row + rows] for weight, row, rows in pieces]
            rows = parts[0] if len(parts) == 1 else jnp.concatenate(parts, axis=0)
            part = jnp.dot(
                context[source][:, column : column + rows.shape[0]],
                rows,
                preferred_element_type=jnp.float32,
            )
            total = part if total is None else total + part
        out_ref[slot] = total.astype(out_ref.dtype)
        if choice:

            @pl.when(block_of(choice[slot]) // 4 != lax.axis_index("tensor"))
            def _():
                refs[-1][0] = total.astype(out_ref.dtype)


def project(context, weights, plan, kind, bases=(), choice=None):
    rows = context[0].shape[0]
    depth = sum(piece[-1] for block in plan for product in block for piece in product[-1])
    vmem = pl.BlockSpec(memory_space=pltpu.VMEM)
    return pl.pallas_call(
        functools.partial(project_kernel, plan, len(context), len(weights), choice),
        out_shape=[
            jax.ShapeDtypeStruct((blocks, rows, CHUNK), kind)
            for blocks in ((len(plan), 1) if choice else (len(plan),))
        ],
        in_specs=[vmem] * (len(context) + len(weights) + len(bases)),
        out_specs=[vmem] * (2 if choice else 1),
        compiler_params=pltpu.CompilerParams(vmem_limit_bytes=12 << 20),
        cost_estimate=pl.CostEstimate(
            flops=2 * rows * depth * CHUNK,
            bytes_accessed=2 * (len(plan) * rows * CHUNK + depth * CHUNK),
            transcendentals=0,
        ),
    )(*context, *weights, *bases)


def live_kernel(counts_ref, donors_ref, after_ref, out_ref):
    my_group = lax.axis_index("dp")
    second = donors_ref[0] == my_group
    for at in range(1, donors_ref.shape[0]):
        second = jnp.logical_or(second, donors_ref[at] == my_group)
    for slot, lives in enumerate((counts_ref[0] >= 1, second)):
        rows = jnp.full((LIVE_ROWS, CHUNK), jnp.where(lives, 1.0, 0.0), jnp.float32)
        out_ref[slot * LIVE_ROWS : (slot + 1) * LIVE_ROWS] = rows.astype(jnp.bfloat16)


def live_slots(counts, donors, after):
    smem = pl.BlockSpec(memory_space=pltpu.SMEM)
    return pl.pallas_call(
        live_kernel,
        out_shape=jax.ShapeDtypeStruct((2 * LIVE_ROWS, CHUNK), jnp.bfloat16),
        in_specs=[smem, smem, pl.BlockSpec(memory_space=pl.ANY)],
        out_specs=pl.BlockSpec(memory_space=pltpu.VMEM),
        compiler_params=pltpu.CompilerParams(vmem_limit_bytes=4 << 20),
    )(counts, donors, after)


def finish_kernel(distances, live_ref, *refs):
    n = len(distances)
    kept, other = refs[:n], refs[n : 2 * n]
    out_ref, buffer, sem = refs[-3:]
    slots, tokens = out_ref.shape[:2]
    tensor = lax.axis_index("tensor")
    steps = []
    for array, group in enumerate(distances):
        several = other[array].shape[0] > 1
        for slot, distance in enumerate(group):
            at = len(steps)
            block = block_of(distance)
            column = pl.multiple_of(block % 4 * CHUNK, CHUNK)
            copies = [
                pltpu.make_async_copy(
                    buffer.at[at, passage],
                    out_ref.at[passage, :, pl.ds(column, CHUNK)],
                    sem.at[at, passage],
                )
                for passage in range(slots)
            ]
            steps.append((block // 4 == tensor, copies))

            @pl.when(block // 4 == tensor)
            def _():
                for passage in range(slots):
                    rows = slice(passage * tokens, (passage + 1) * tokens)
                    both = kept[array][slot, rows] + other[array][slot if several else 0, rows]
                    live = live_ref[passage * LIVE_ROWS : passage * LIVE_ROWS + 1]
                    buffer[at, passage] = both * jnp.broadcast_to(live, both.shape)
                    copies[passage].start()

    for mine, copies in steps:

        @pl.when(mine)
        def _():
            for copy in copies:
                copy.wait()


def finish(kept, other, distances, live, slots, held=()):
    rows = kept[0].shape[1]
    tokens = rows // slots
    vmem = pl.BlockSpec(memory_space=pltpu.VMEM)
    away = pl.BlockSpec(memory_space=pl.ANY)
    blocks = sum(len(group) for group in distances)
    n_in = 1 + 2 * len(kept)
    return pl.pallas_call(
        functools.partial(finish_kernel, distances),
        out_shape=jax.ShapeDtypeStruct((slots, tokens, 4 * CHUNK), jnp.bfloat16),
        in_specs=[vmem] * n_in + [away] * len(held),
        out_specs=away,
        scratch_shapes=[
            pltpu.VMEM((blocks, slots, tokens, CHUNK), jnp.bfloat16),
            pltpu.SemaphoreType.DMA((blocks, slots)),
        ],
        input_output_aliases={n_in: 0} if held else {},
        compiler_params=pltpu.CompilerParams(vmem_limit_bytes=12 << 20),
        cost_estimate=pl.CostEstimate(
            flops=blocks * rows * CHUNK,
            bytes_accessed=blocks * rows * CHUNK * 3,
            transcendentals=0,
        ),
    )(live, *kept, *other, *held)


def with_ring(queries, key_rows, values, position_bias, out_weight, counts, donors, reps, dp_size):
    slots = queries.shape[0]
    ahead = ring_pairs(reps, dp_size, 1)
    back = ring_pairs(reps, dp_size, -1)
    places = [(r, d, t) for r in range(2) for d in range(dp_size) for t in range(2)]
    across = [
        (device_index(r, d, t, dp_size), device_index(1 - r, d, t, dp_size)) for r, d, t in places
    ]
    cores = [
        (device_index(r, d, t, dp_size), device_index(r, d, 1 - t, dp_size)) for r, d, t in places
    ]
    send = lambda value, pairs: lax.ppermute(value, AXES, pairs)
    depth = out_weight.shape[0]
    half, cut = depth // 2, 11 * depth // 32
    over = half - cut
    lead = over // 128 * 128
    spill = over - lead
    edge = lambda p, q: jnp.concatenate([p[:cut], q[-cut:]], axis=0)
    barrier = lax.optimization_barrier

    p1, q1 = send(out_weight[:-cut], ahead), send(out_weight[cut:], back)
    c0 = attend(queries, key_rows, values, position_bias, 0, 2)
    p1, c0 = barrier((p1, c0))

    p2, q2, y1 = send(p1, ahead), send(q1, back), send(edge(p1, q1), across)
    c1 = attend(queries, key_rows, values, position_bias, 2, 1, (c0,))
    live = live_slots(counts, donors, c0)
    p2, c1 = barrier((p2, c1))
    q2, live = barrier((q2, live))

    p3, q3, y2 = send(p2, ahead), send(q2, back), send(edge(p2, q2), across)
    c1 = attend(queries, key_rows, values, position_bias, 3, 1, (c1,), joined=True)
    p3, q3, y1, c1 = barrier((p3, q3, y1, c1))
    context = (c0, c1)

    own = [(0, 0, [(0, 0, half)]), (1, 0, [(0, half, half)])]
    p_block = lambda p, y: [(0, 0, [(p, 0, half)]), (1, 0, [(p, half, over), (y, cut, cut)])]
    q_block = lambda q, y: [(0, 0, [(y, 0, cut), (q, 0, over)]), (1, 0, [(q, over, half)])]
    p_part = [(0, 0, [(0, 0, half)]), (1, 0, [(0, half, lead)])]
    q_part = [(0, half - lead, [(1, spill, lead)]), (1, 0, [(1, over, half)])]
    p_rest = [(1, lead, [(0, half + lead, spill), (2, cut, cut)])]
    q_rest = [(0, 0, [(2, 0, cut), (1, 0, spill)])]
    opposite = [(0, 0, [(3, 0, half)]), (1, 0, [(4, 0, half)])]

    p4, q4 = send(p3[:half], ahead), send(q3[-half:], back)
    y3 = send(edge(p3, q3), across)
    (e1,) = project(
        context, (out_weight, p1, q1, y1), [own, p_block(1, 3), q_block(2, 3)], jnp.bfloat16
    )
    e2, s2 = project(
        context, (p2, q2, y2), [p_block(0, 2), q_block(1, 2)], jnp.bfloat16, choice=(2, -2)
    )
    (started,) = project(context, (p3, q3), [p_part, q_part], jnp.float32)
    p4, q4, y3, e2, s2, started = barrier((p4, q4, y3, e2, s2, started))

    x1, x2 = send(e1, cores), send(s2, cores)
    (e3,) = project(
        context, (p3, q3, y3, p4, q4), [p_rest, q_rest, opposite], jnp.bfloat16, (started,)
    )
    x3 = send(e3, cores)
    early = finish((e1,), (x1,), ((0, 1, -1),), live, slots)
    x2, x3, early = barrier((x2, x3, early))
    return finish((e2, e3), (x2, x3), ((2, -2), (3, -3, 4)), live, slots, (early,))


def with_gather(queries, key_rows, values, position_bias, out_weight, counts, donors):
    slots, tokens, features = queries.shape
    whole = lax.all_gather(out_weight, "dp", axis=1, tiled=True)
    context = attend(queries, key_rows, values, position_bias, 0, features // CHUNK)
    product = jnp.dot(context, whole, preferred_element_type=jnp.float32).astype(jnp.bfloat16)
    merged = lax.psum_scatter(product, "tensor", scatter_dimension=1, tiled=True)
    first_live = counts[0] >= 1
    second_live = jnp.any(donors == lax.axis_index("dp"))
    live = jnp.stack([first_live, second_live]).astype(jnp.bfloat16)
    return merged.reshape(slots, tokens, merged.shape[1]) * live[:, None, None]


def solution(mesh):
    in_specs = (
        P(("rep", "dp"), None, "tensor"),
        P(("rep", "dp"), None, "tensor"),
        P(("rep", "dp"), None, "tensor"),
        P(None, "tensor"),
        P("tensor", "dp"),
        P(("rep", "dp")),
        P("rep"),
    )
    out_specs = P(("rep", "dp"), None, "tensor")
    reps, dp_size = mesh.shape["rep"], mesh.shape["dp"]
    if reps == 2 and dp_size == 8 and mesh.shape["tensor"] == 2:
        on_device = functools.partial(with_ring, reps=reps, dp_size=dp_size)
    else:
        on_device = with_gather
    return jax.shard_map(
        on_device, mesh=mesh, in_specs=in_specs, out_specs=out_specs, check_vma=False
    )
```

```python
import functools

import jax
import jax.numpy as jnp
from jax import lax
from jax.experimental import pallas as pl
from jax.experimental.pallas import tpu as pltpu
from jax.sharding import PartitionSpec as P

HEAD_DIM = 64
PAIR = 2 * HEAD_DIM
CHUNK = 256
LIVE_ROWS = 16
THRESHOLDS = (12, 16, 23, 32, 46, 64, 91)
AXES = ("rep", "dp", "tensor")


def bias_rows(position_bias, tokens):
    bucket_count = position_bias.shape[1]
    shape = (bucket_count, 2 * tokens)
    relative = lax.broadcasted_iota(jnp.int32, shape, 1) - (tokens - 1)
    distance = jnp.abs(relative)
    far = jnp.full(shape, 8, jnp.int32)
    for threshold in THRESHOLDS:
        far = far + jnp.where(distance >= threshold, 1, 0)
    bucket = jnp.where(distance < 8, distance, far) + jnp.where(relative > 0, 16, 0)
    one_hot = jnp.where(bucket == lax.broadcasted_iota(jnp.int32, shape, 0), 1.0, 0.0)
    return lax.dot_general(
        position_bias,
        one_hot,
        (((1,), (0,)), ((), ())),
        precision=lax.Precision.HIGHEST,
        preferred_element_type=jnp.float32,
    )


def attention_kernel(first, joined, bias_ref, *refs):
    sources, (out_ref, held, sem) = refs[:3], refs[-3:]
    count, _, slots, tokens, width = held.shape
    offset = out_ref.shape[1] - count * width
    copies = [
        [
            pltpu.make_async_copy(
                source.at[:, :, (first + chunk) * width : (first + chunk + 1) * width],
                held.at[chunk, at],
                sem.at[chunk, at],
            )
            for at, source in enumerate(sources)
        ]
        for chunk in range(count)
    ]
    for chunk in copies:
        for copy in chunk:
            copy.start()
    if joined:
        out_ref[:, :offset] = refs[3][...]
    rows = bias_rows(bias_ref[...], tokens)
    lower = lax.broadcasted_iota(jnp.int32, (tokens, PAIR), 1) < HEAD_DIM
    for chunk in range(count):
        for copy in copies[chunk]:
            copy.wait()
        for pair in range(width // PAIR):
            columns = slice(pair * PAIR, (pair + 1) * PAIR)
            head = (first + chunk) * (width // HEAD_DIM) + 2 * pair
            terms = [toeplitz(rows[head + i : head + i + 1], tokens) for i in range(2)]
            for slot in range(slots):
                query, key, value = (held[chunk, at, slot, :, columns] for at in range(3))
                sums = []
                for i in range(2):
                    own = lower if i == 0 else jnp.logical_not(lower)
                    scores = lax.dot_general(
                        query,
                        jnp.where(own, key, 0),
                        (((1,), (1,)), ((), ())),
                        preferred_element_type=jnp.float32,
                    )
                    scores = scores + terms[i]
                    highest = jnp.max(scores, axis=-1, keepdims=True)
                    expd = jnp.exp(scores - highest).astype(jnp.bfloat16)
                    sums.append(
                        jnp.dot(expd, jnp.where(own, value, 1), preferred_element_type=jnp.float32)
                    )
                weighted = jnp.where(lower, sums[0], sums[1])
                total = pltpu.roll(jnp.where(lower, sums[1], sums[0]), HEAD_DIM, 1)
                at = offset + chunk * width + pair * PAIR
                at = slice(at, at + PAIR)
                out_ref[slot * tokens : (slot + 1) * tokens, at] = (weighted / total).astype(
                    jnp.bfloat16
                )


def toeplitz(row, tokens):
    spread = jnp.broadcast_to(row, (8, 2 * tokens))
    base = pltpu.roll(spread, tokens + 1, 1, stride=1, stride_axis=0)
    rolled = [base if i == 0 else pltpu.roll(base, 8 * i, 1) for i in range(16)]
    groups = []
    for group in range(tokens // 8):
        turned, whole = rolled[group % 16], group // 16 * 128
        if whole:
            turned = jnp.concatenate([turned[:, -whole:], turned[:, : tokens - whole]], axis=1)
        groups.append(turned[:, :tokens])
    return jnp.concatenate(groups, axis=0)


def attend(queries, key_rows, values, position_bias, first, count, after=(), joined=False):
    slots, tokens, _ = queries.shape
    vmem = pl.BlockSpec(memory_space=pltpu.VMEM)
    away = pl.BlockSpec(memory_space=pltpu.HBM)
    last = vmem if joined else pl.BlockSpec(memory_space=pl.ANY)
    columns = CHUNK * count + (after[0].shape[1] if joined else 0)
    scores = slots * (CHUNK // HEAD_DIM) * tokens * tokens * count
    return pl.pallas_call(
        functools.partial(attention_kernel, first, joined),
        out_shape=jax.ShapeDtypeStruct((slots * tokens, columns), jnp.bfloat16),
        in_specs=[vmem] + [away] * 3 + [last] * len(after),
        out_specs=vmem,
        scratch_shapes=[
            pltpu.VMEM((count, 3, slots, tokens, CHUNK), jnp.bfloat16),
            pltpu.SemaphoreType.DMA((count, 3)),
        ],
        compiler_params=pltpu.CompilerParams(vmem_limit_bytes=14 << 20),
        cost_estimate=pl.CostEstimate(
            flops=4 * scores * HEAD_DIM,
            bytes_accessed=8 * slots * tokens * CHUNK * count,
            transcendentals=scores,
        ),
    )(position_bias.T, queries, key_rows, values, *after)


def device_index(rep, dp, tensor, dp_size):
    return (rep * dp_size + dp) * 2 + tensor


def ring_order(dp_size):
    half = dp_size // 2
    return [2 * i for i in range(half)] + [2 * i + 1 for i in reversed(range(half))]


def ring_pairs(reps, dp_size, way):
    order = ring_order(dp_size)
    pairs = []
    for rep in range(reps):
        step = way if rep == 0 else -way
        for place in range(dp_size):
            to = order[(place + step) % dp_size]
            for tensor in range(2):
                pairs.append(
                    (
                        device_index(rep, order[place], tensor, dp_size),
                        device_index(rep, to, tensor, dp_size),
                    )
                )
    return pairs


def block_of(distance):
    dp = lax.axis_index("dp")
    place = jnp.where(dp % 2 == 0, dp // 2, 7 - dp // 2)
    way = jnp.where(lax.axis_index("rep") == 0, 1, -1)
    place = (place - way * distance + 16) % 8
    return jnp.where(place < 4, 2 * place, 2 * (7 - place) + 1)


def project_kernel(plan, n_context, n_weights, choice, *refs):
    context = refs[:n_context]
    weights = refs[n_context : n_context + n_weights]
    n_out = 2 if choice else 1
    bases, out_ref = refs[n_context + n_weights : -n_out], refs[-n_out]
    for slot, products in enumerate(plan):
        total = bases[0][slot] if bases and slot < bases[0].shape[0] else None
        for source, column, pieces in products:
            parts = [weights[weight][row : row + rows] for weight, row, rows in pieces]
            rows = parts[0] if len(parts) == 1 else jnp.concatenate(parts, axis=0)
            part = jnp.dot(
                context[source][:, column : column + rows.shape[0]],
                rows,
                preferred_element_type=jnp.float32,
            )
            total = part if total is None else total + part
        out_ref[slot] = total.astype(out_ref.dtype)
        if choice:

            @pl.when(block_of(choice[slot]) // 4 != lax.axis_index("tensor"))
            def _():
                refs[-1][0] = total.astype(out_ref.dtype)


def project(context, weights, plan, kind, bases=(), choice=None):
    rows = context[0].shape[0]
    depth = sum(piece[-1] for block in plan for product in block for piece in product[-1])
    vmem = pl.BlockSpec(memory_space=pltpu.VMEM)
    return pl.pallas_call(
        functools.partial(project_kernel, plan, len(context), len(weights), choice),
        out_shape=[
            jax.ShapeDtypeStruct((blocks, rows, CHUNK), kind)
            for blocks in ((len(plan), 1) if choice else (len(plan),))
        ],
        in_specs=[vmem] * (len(context) + len(weights) + len(bases)),
        out_specs=[vmem] * (2 if choice else 1),
        compiler_params=pltpu.CompilerParams(vmem_limit_bytes=12 << 20),
        cost_estimate=pl.CostEstimate(
            flops=2 * rows * depth * CHUNK,
            bytes_accessed=2 * (len(plan) * rows * CHUNK + depth * CHUNK),
            transcendentals=0,
        ),
    )(*context, *weights, *bases)


def live_kernel(counts_ref, donors_ref, after_ref, out_ref):
    my_group = lax.axis_index("dp")
    second = donors_ref[0] == my_group
    for at in range(1, donors_ref.shape[0]):
        second = jnp.logical_or(second, donors_ref[at] == my_group)
    for slot, lives in enumerate((counts_ref[0] >= 1, second)):
        rows = jnp.full((LIVE_ROWS, CHUNK), jnp.where(lives, 1.0, 0.0), jnp.float32)
        out_ref[slot * LIVE_ROWS : (slot + 1) * LIVE_ROWS] = rows.astype(jnp.bfloat16)


def live_slots(counts, donors, after):
    smem = pl.BlockSpec(memory_space=pltpu.SMEM)
    return pl.pallas_call(
        live_kernel,
        out_shape=jax.ShapeDtypeStruct((2 * LIVE_ROWS, CHUNK), jnp.bfloat16),
        in_specs=[smem, smem, pl.BlockSpec(memory_space=pl.ANY)],
        out_specs=pl.BlockSpec(memory_space=pltpu.VMEM),
        compiler_params=pltpu.CompilerParams(vmem_limit_bytes=4 << 20),
    )(counts, donors, after)


def finish_kernel(distances, live_ref, *refs):
    n = len(distances)
    kept, other = refs[:n], refs[n : 2 * n]
    out_ref, buffer, sem = refs[-3:]
    slots, tokens = out_ref.shape[:2]
    tensor = lax.axis_index("tensor")
    steps = []
    for array, group in enumerate(distances):
        several = other[array].shape[0] > 1
        for slot, distance in enumerate(group):
            at = len(steps)
            block = block_of(distance)
            column = pl.multiple_of(block % 4 * CHUNK, CHUNK)
            copies = [
                pltpu.make_async_copy(
                    buffer.at[at, passage],
                    out_ref.at[passage, :, pl.ds(column, CHUNK)],
                    sem.at[at, passage],
                )
                for passage in range(slots)
            ]
            steps.append((block // 4 == tensor, copies))

            @pl.when(block // 4 == tensor)
            def _():
                for passage in range(slots):
                    rows = slice(passage * tokens, (passage + 1) * tokens)
                    both = kept[array][slot, rows] + other[array][slot if several else 0, rows]
                    live = live_ref[passage * LIVE_ROWS : passage * LIVE_ROWS + 1]
                    buffer[at, passage] = both * jnp.broadcast_to(live, both.shape)
                    copies[passage].start()

    for mine, copies in steps:

        @pl.when(mine)
        def _():
            for copy in copies:
                copy.wait()


def finish(kept, other, distances, live, slots, held=()):
    rows = kept[0].shape[1]
    tokens = rows // slots
    vmem = pl.BlockSpec(memory_space=pltpu.VMEM)
    away = pl.BlockSpec(memory_space=pl.ANY)
    blocks = sum(len(group) for group in distances)
    n_in = 1 + 2 * len(kept)
    return pl.pallas_call(
        functools.partial(finish_kernel, distances),
        out_shape=jax.ShapeDtypeStruct((slots, tokens, 4 * CHUNK), jnp.bfloat16),
        in_specs=[vmem] * n_in + [away] * len(held),
        out_specs=away,
        scratch_shapes=[
            pltpu.VMEM((blocks, slots, tokens, CHUNK), jnp.bfloat16),
            pltpu.SemaphoreType.DMA((blocks, slots)),
        ],
        input_output_aliases={n_in: 0} if held else {},
        compiler_params=pltpu.CompilerParams(vmem_limit_bytes=12 << 20),
        cost_estimate=pl.CostEstimate(
            flops=blocks * rows * CHUNK,
            bytes_accessed=blocks * rows * CHUNK * 3,
            transcendentals=0,
        ),
    )(live, *kept, *other, *held)


def with_ring(queries, key_rows, values, position_bias, out_weight, counts, donors, reps, dp_size):
    slots = queries.shape[0]
    ahead = ring_pairs(reps, dp_size, 1)
    back = ring_pairs(reps, dp_size, -1)
    places = [(r, d, t) for r in range(2) for d in range(dp_size) for t in range(2)]
    across = [
        (device_index(r, d, t, dp_size), device_index(1 - r, d, t, dp_size)) for r, d, t in places
    ]
    cores = [
        (device_index(r, d, t, dp_size), device_index(r, d, 1 - t, dp_size)) for r, d, t in places
    ]
    send = lambda value, pairs: lax.ppermute(value, AXES, pairs)
    depth = out_weight.shape[0]
    half, cut = depth // 2, 11 * depth // 32
    over = half - cut
    lead = over // 128 * 128
    spill = over - lead
    edge = lambda p, q: jnp.concatenate([p[:cut], q[-cut:]], axis=0)
    barrier = lax.optimization_barrier

    p1, q1 = send(out_weight[:-cut], ahead), send(out_weight[cut:], back)
    c0 = attend(queries, key_rows, values, position_bias, 0, 2)
    p1, c0 = barrier((p1, c0))

    p2, q2, y1 = send(p1, ahead), send(q1, back), send(edge(p1, q1), across)
    c1 = attend(queries, key_rows, values, position_bias, 2, 1, (c0,))
    live = live_slots(counts, donors, c0)
    p2, c1, live = barrier((p2, c1, live))

    p3, q3, y2 = send(p2, ahead), send(q2, back), send(edge(p2, q2), across)
    c1 = attend(queries, key_rows, values, position_bias, 3, 1, (c1,), joined=True)
    p3, q3, y1, c1 = barrier((p3, q3, y1, c1))
    context = (c0, c1)

    own = [(0, 0, [(0, 0, half)]), (1, 0, [(0, half, half)])]
    p_block = lambda p, y: [(0, 0, [(p, 0, half)]), (1, 0, [(p, half, over), (y, cut, cut)])]
    q_block = lambda q, y: [(0, 0, [(y, 0, cut), (q, 0, over)]), (1, 0, [(q, over, half)])]
    p_part = [(0, 0, [(0, 0, half)]), (1, 0, [(0, half, lead)])]
    q_part = [(0, half - lead, [(1, spill, lead)]), (1, 0, [(1, over, half)])]
    p_rest = [(1, lead, [(0, half + lead, spill), (2, cut, cut)])]
    q_rest = [(0, 0, [(2, 0, cut), (1, 0, spill)])]
    opposite = [(0, 0, [(0, 0, half)]), (1, 0, [(1, 0, half)])]

    p4, q4 = send(p3[:half], ahead), send(q3[-half:], back)
    y3 = send(edge(p3, q3), across)
    (e1,) = project(
        context, (out_weight, p1, q1, y1), [own, p_block(1, 3), q_block(2, 3)], jnp.bfloat16
    )
    e2, s2 = project(
        context, (p2, q2, y2), [p_block(0, 2), q_block(1, 2)], jnp.bfloat16, choice=(2, -2)
    )
    (started,) = project(context, (p3, q3), [p_part, q_part], jnp.float32)
    p4, q4, e2, s2, started = barrier((p4, q4, e2, s2, started))

    (e4,) = project(context, (p4, q4), [opposite], jnp.bfloat16)
    x1, x2, x4 = send(e1, cores), send(s2, cores), send(e4, cores)
    y3, e4 = barrier((y3, e4))
    (e3,) = project(context, (p3, q3, y3), [p_rest, q_rest], jnp.bfloat16, (started,))
    x3 = send(e3, cores)
    early = finish((e1,), (x1,), ((0, 1, -1),), live, slots)
    x2, x3, x4, early = barrier((x2, x3, x4, early))
    return finish(
        (e2, e4, e3), (x2, x4, x3), ((2, -2), (4,), (3, -3)), live, slots, (early,)
    )


def with_gather(queries, key_rows, values, position_bias, out_weight, counts, donors):
    slots, tokens, features = queries.shape
    whole = lax.all_gather(out_weight, "dp", axis=1, tiled=True)
    context = attend(queries, key_rows, values, position_bias, 0, features // CHUNK)
    product = jnp.dot(context, whole, preferred_element_type=jnp.float32).astype(jnp.bfloat16)
    merged = lax.psum_scatter(product, "tensor", scatter_dimension=1, tiled=True)
    first_live = counts[0] >= 1
    second_live = jnp.any(donors == lax.axis_index("dp"))
    live = jnp.stack([first_live, second_live]).astype(jnp.bfloat16)
    return merged.reshape(slots, tokens, merged.shape[1]) * live[:, None, None]


def solution(mesh):
    in_specs = (
        P(("rep", "dp"), None, "tensor"),
        P(("rep", "dp"), None, "tensor"),
        P(("rep", "dp"), None, "tensor"),
        P(None, "tensor"),
        P("tensor", "dp"),
        P(("rep", "dp")),
        P("rep"),
    )
    out_specs = P(("rep", "dp"), None, "tensor")
    reps, dp_size = mesh.shape["rep"], mesh.shape["dp"]
    if reps == 2 and dp_size == 8 and mesh.shape["tensor"] == 2:
        on_device = functools.partial(with_ring, reps=reps, dp_size=dp_size)
    else:
        on_device = with_gather
    return jax.shard_map(
        on_device, mesh=mesh, in_specs=in_specs, out_specs=out_specs, check_vma=False
    )
```

```python
import functools

import jax
import jax.numpy as jnp
from jax import lax
from jax.experimental import pallas as pl
from jax.experimental.pallas import tpu as pltpu
from jax.sharding import PartitionSpec as P

HEAD_DIM = 64
PAIR = 2 * HEAD_DIM
CHUNK = 256
LIVE_ROWS = 16
THRESHOLDS = (12, 16, 23, 32, 46, 64, 91)
AXES = ("rep", "dp", "tensor")


def bias_rows(position_bias, tokens):
    bucket_count = position_bias.shape[1]
    shape = (bucket_count, 2 * tokens)
    relative = lax.broadcasted_iota(jnp.int32, shape, 1) - (tokens - 1)
    distance = jnp.abs(relative)
    far = jnp.full(shape, 8, jnp.int32)
    for threshold in THRESHOLDS:
        far = far + jnp.where(distance >= threshold, 1, 0)
    bucket = jnp.where(distance < 8, distance, far) + jnp.where(relative > 0, 16, 0)
    one_hot = jnp.where(bucket == lax.broadcasted_iota(jnp.int32, shape, 0), 1.0, 0.0)
    return lax.dot_general(
        position_bias,
        one_hot,
        (((1,), (0,)), ((), ())),
        precision=lax.Precision.HIGHEST,
        preferred_element_type=jnp.float32,
    )


def attention_kernel(first, joined, bias_ref, *refs):
    sources, (out_ref, held, sem) = refs[:3], refs[-3:]
    count, _, slots, tokens, width = held.shape
    offset = out_ref.shape[1] - count * width
    copies = [
        [
            pltpu.make_async_copy(
                source.at[:, :, (first + chunk) * width : (first + chunk + 1) * width],
                held.at[chunk, at],
                sem.at[chunk, at],
            )
            for at, source in enumerate(sources)
        ]
        for chunk in range(count)
    ]
    for chunk in copies:
        for copy in chunk:
            copy.start()
    if joined:
        out_ref[:, :offset] = refs[3][...]
    rows = bias_rows(bias_ref[...], tokens)
    lower = lax.broadcasted_iota(jnp.int32, (tokens, PAIR), 1) < HEAD_DIM
    for chunk in range(count):
        for copy in copies[chunk]:
            copy.wait()
        for pair in range(width // PAIR):
            columns = slice(pair * PAIR, (pair + 1) * PAIR)
            head = (first + chunk) * (width // HEAD_DIM) + 2 * pair
            terms = [toeplitz(rows[head + i : head + i + 1], tokens) for i in range(2)]
            for slot in range(slots):
                query, key, value = (held[chunk, at, slot, :, columns] for at in range(3))
                sums = []
                for i in range(2):
                    own = lower if i == 0 else jnp.logical_not(lower)
                    scores = lax.dot_general(
                        query,
                        jnp.where(own, key, 0),
                        (((1,), (1,)), ((), ())),
                        preferred_element_type=jnp.float32,
                    )
                    scores = scores + terms[i]
                    highest = jnp.max(scores, axis=-1, keepdims=True)
                    expd = jnp.exp(scores - highest).astype(jnp.bfloat16)
                    sums.append(
                        jnp.dot(expd, jnp.where(own, value, 1), preferred_element_type=jnp.float32)
                    )
                weighted = jnp.where(lower, sums[0], sums[1])
                total = pltpu.roll(jnp.where(lower, sums[1], sums[0]), HEAD_DIM, 1)
                at = offset + chunk * width + pair * PAIR
                at = slice(at, at + PAIR)
                out_ref[slot * tokens : (slot + 1) * tokens, at] = (weighted / total).astype(
                    jnp.bfloat16
                )


def toeplitz(row, tokens):
    spread = jnp.broadcast_to(row, (8, 2 * tokens))
    base = pltpu.roll(spread, tokens + 1, 1, stride=1, stride_axis=0)
    rolled = [base if i == 0 else pltpu.roll(base, 8 * i, 1) for i in range(16)]
    groups = []
    for group in range(tokens // 8):
        turned, whole = rolled[group % 16], group // 16 * 128
        if whole:
            turned = jnp.concatenate([turned[:, -whole:], turned[:, : tokens - whole]], axis=1)
        groups.append(turned[:, :tokens])
    return jnp.concatenate(groups, axis=0)


def attend(queries, key_rows, values, position_bias, first, count, after=(), joined=False):
    slots, tokens, _ = queries.shape
    vmem = pl.BlockSpec(memory_space=pltpu.VMEM)
    away = pl.BlockSpec(memory_space=pltpu.HBM)
    last = vmem if joined else pl.BlockSpec(memory_space=pl.ANY)
    columns = CHUNK * count + (after[0].shape[1] if joined else 0)
    scores = slots * (CHUNK // HEAD_DIM) * tokens * tokens * count
    return pl.pallas_call(
        functools.partial(attention_kernel, first, joined),
        out_shape=jax.ShapeDtypeStruct((slots * tokens, columns), jnp.bfloat16),
        in_specs=[vmem] + [away] * 3 + [last] * len(after),
        out_specs=vmem,
        scratch_shapes=[
            pltpu.VMEM((count, 3, slots, tokens, CHUNK), jnp.bfloat16),
            pltpu.SemaphoreType.DMA((count, 3)),
        ],
        compiler_params=pltpu.CompilerParams(vmem_limit_bytes=14 << 20),
        cost_estimate=pl.CostEstimate(
            flops=4 * scores * HEAD_DIM,
            bytes_accessed=8 * slots * tokens * CHUNK * count,
            transcendentals=scores,
        ),
    )(position_bias.T, queries, key_rows, values, *after)


def device_index(rep, dp, tensor, dp_size):
    return (rep * dp_size + dp) * 2 + tensor


def ring_order(dp_size):
    half = dp_size // 2
    return [2 * i for i in range(half)] + [2 * i + 1 for i in reversed(range(half))]


def ring_pairs(reps, dp_size, way):
    order = ring_order(dp_size)
    pairs = []
    for rep in range(reps):
        step = way if rep == 0 else -way
        for place in range(dp_size):
            to = order[(place + step) % dp_size]
            for tensor in range(2):
                pairs.append(
                    (
                        device_index(rep, order[place], tensor, dp_size),
                        device_index(rep, to, tensor, dp_size),
                    )
                )
    return pairs


def block_of(distance):
    dp = lax.axis_index("dp")
    place = jnp.where(dp % 2 == 0, dp // 2, 7 - dp // 2)
    way = jnp.where(lax.axis_index("rep") == 0, 1, -1)
    place = (place - way * distance + 16) % 8
    return jnp.where(place < 4, 2 * place, 2 * (7 - place) + 1)


def project_kernel(plan, n_context, n_weights, choice, taken, *refs):
    context = refs[:n_context]
    weights = refs[n_context : n_context + n_weights]
    n_out = 2 if choice else 1
    bases, out_ref = refs[n_context + n_weights : -n_out], refs[-n_out]
    if taken:
        out_ref[len(plan)] = bases[-1][0]
        bases = bases[:-1]
    for slot, products in enumerate(plan):
        total = bases[0][slot] if bases and slot < bases[0].shape[0] else None
        for source, column, pieces in products:
            parts = [weights[weight][row : row + rows] for weight, row, rows in pieces]
            rows = parts[0] if len(parts) == 1 else jnp.concatenate(parts, axis=0)
            part = jnp.dot(
                context[source][:, column : column + rows.shape[0]],
                rows,
                preferred_element_type=jnp.float32,
            )
            total = part if total is None else total + part
        out_ref[slot] = total.astype(out_ref.dtype)
        if choice:

            @pl.when(block_of(choice[slot]) // 4 != lax.axis_index("tensor"))
            def _():
                refs[-1][0] = total.astype(out_ref.dtype)


def project(context, weights, plan, kind, bases=(), choice=None, taken=()):
    rows = context[0].shape[0]
    depth = sum(piece[-1] for block in plan for product in block for piece in product[-1])
    vmem = pl.BlockSpec(memory_space=pltpu.VMEM)
    return pl.pallas_call(
        functools.partial(project_kernel, plan, len(context), len(weights), choice, bool(taken)),
        out_shape=[
            jax.ShapeDtypeStruct((blocks, rows, CHUNK), kind)
            for blocks in ((len(plan), 1) if choice else (len(plan) + len(taken),))
        ],
        in_specs=[vmem] * (len(context) + len(weights) + len(bases) + len(taken)),
        out_specs=[vmem] * (2 if choice else 1),
        compiler_params=pltpu.CompilerParams(vmem_limit_bytes=12 << 20),
        cost_estimate=pl.CostEstimate(
            flops=2 * rows * depth * CHUNK,
            bytes_accessed=2 * (len(plan) * rows * CHUNK + depth * CHUNK),
            transcendentals=0,
        ),
    )(*context, *weights, *bases, *taken)


def live_kernel(counts_ref, donors_ref, after_ref, out_ref):
    my_group = lax.axis_index("dp")
    second = donors_ref[0] == my_group
    for at in range(1, donors_ref.shape[0]):
        second = jnp.logical_or(second, donors_ref[at] == my_group)
    for slot, lives in enumerate((counts_ref[0] >= 1, second)):
        rows = jnp.full((LIVE_ROWS, CHUNK), jnp.where(lives, 1.0, 0.0), jnp.float32)
        out_ref[slot * LIVE_ROWS : (slot + 1) * LIVE_ROWS] = rows.astype(jnp.bfloat16)


def live_slots(counts, donors, after):
    smem = pl.BlockSpec(memory_space=pltpu.SMEM)
    return pl.pallas_call(
        live_kernel,
        out_shape=jax.ShapeDtypeStruct((2 * LIVE_ROWS, CHUNK), jnp.bfloat16),
        in_specs=[smem, smem, pl.BlockSpec(memory_space=pl.ANY)],
        out_specs=pl.BlockSpec(memory_space=pltpu.VMEM),
        compiler_params=pltpu.CompilerParams(vmem_limit_bytes=4 << 20),
    )(counts, donors, after)


def finish_kernel(distances, live_ref, *refs):
    n = len(distances)
    kept, other = refs[:n], refs[n : 2 * n]
    out_ref, buffer, sem = refs[-3:]
    slots, tokens = out_ref.shape[:2]
    tensor = lax.axis_index("tensor")
    steps = []
    for array, group in enumerate(distances):
        for slot, (distance, theirs) in enumerate(group):
            at = len(steps)
            block = block_of(distance)
            column = pl.multiple_of(block % 4 * CHUNK, CHUNK)
            copies = [
                pltpu.make_async_copy(
                    buffer.at[at, passage],
                    out_ref.at[passage, :, pl.ds(column, CHUNK)],
                    sem.at[at, passage],
                )
                for passage in range(slots)
            ]
            steps.append((block // 4 == tensor, copies))

            @pl.when(block // 4 == tensor)
            def _():
                for passage in range(slots):
                    rows = slice(passage * tokens, (passage + 1) * tokens)
                    both = kept[array][slot, rows] + other[array][theirs, rows]
                    live = live_ref[passage * LIVE_ROWS : passage * LIVE_ROWS + 1]
                    buffer[at, passage] = both * jnp.broadcast_to(live, both.shape)
                    copies[passage].start()

    for mine, copies in steps:

        @pl.when(mine)
        def _():
            for copy in copies:
                copy.wait()


def finish(kept, other, distances, live, slots, held=()):
    rows = kept[0].shape[1]
    tokens = rows // slots
    vmem = pl.BlockSpec(memory_space=pltpu.VMEM)
    away = pl.BlockSpec(memory_space=pl.ANY)
    blocks = sum(len(group) for group in distances)
    n_in = 1 + 2 * len(kept)
    return pl.pallas_call(
        functools.partial(finish_kernel, distances),
        out_shape=jax.ShapeDtypeStruct((slots, tokens, 4 * CHUNK), jnp.bfloat16),
        in_specs=[vmem] * n_in + [away] * len(held),
        out_specs=away,
        scratch_shapes=[
            pltpu.VMEM((blocks, slots, tokens, CHUNK), jnp.bfloat16),
            pltpu.SemaphoreType.DMA((blocks, slots)),
        ],
        input_output_aliases={n_in: 0} if held else {},
        compiler_params=pltpu.CompilerParams(vmem_limit_bytes=12 << 20),
        cost_estimate=pl.CostEstimate(
            flops=blocks * rows * CHUNK,
            bytes_accessed=blocks * rows * CHUNK * 3,
            transcendentals=0,
        ),
    )(live, *kept, *other, *held)


def with_ring(queries, key_rows, values, position_bias, out_weight, counts, donors, reps, dp_size):
    slots = queries.shape[0]
    ahead = ring_pairs(reps, dp_size, 1)
    back = ring_pairs(reps, dp_size, -1)
    places = [(r, d, t) for r in range(2) for d in range(dp_size) for t in range(2)]
    across = [
        (device_index(r, d, t, dp_size), device_index(1 - r, d, t, dp_size)) for r, d, t in places
    ]
    cores = [
        (device_index(r, d, t, dp_size), device_index(r, d, 1 - t, dp_size)) for r, d, t in places
    ]
    send = lambda value, pairs: lax.ppermute(value, AXES, pairs)
    depth = out_weight.shape[0]
    half, cut = depth // 2, 11 * depth // 32
    over = half - cut
    lead = over // 128 * 128
    spill = over - lead
    edge = lambda p, q: jnp.concatenate([p[:cut], q[-cut:]], axis=0)
    barrier = lax.optimization_barrier

    p1, q1 = send(out_weight[:-cut], ahead), send(out_weight[cut:], back)
    c0 = attend(queries, key_rows, values, position_bias, 0, 2)
    p1, c0 = barrier((p1, c0))

    p2, q2, y1 = send(p1, ahead), send(q1, back), send(edge(p1, q1), across)
    c1 = attend(queries, key_rows, values, position_bias, 2, 1, (c0,))
    live = live_slots(counts, donors, c0)
    p2, c1, live = barrier((p2, c1, live))

    p3, q3, y2 = send(p2, ahead), send(q2, back), send(edge(p2, q2), across)
    c1 = attend(queries, key_rows, values, position_bias, 3, 1, (c1,), joined=True)
    p3, q3, y1, c1 = barrier((p3, q3, y1, c1))
    context = (c0, c1)

    own = [(0, 0, [(0, 0, half)]), (1, 0, [(0, half, half)])]
    p_block = lambda p, y: [(0, 0, [(p, 0, half)]), (1, 0, [(p, half, over), (y, cut, cut)])]
    q_block = lambda q, y: [(0, 0, [(y, 0, cut), (q, 0, over)]), (1, 0, [(q, over, half)])]
    p_part = [(0, 0, [(0, 0, half)]), (1, 0, [(0, half, lead)])]
    q_part = [(0, half - lead, [(1, spill, lead)]), (1, 0, [(1, over, half)])]
    p_rest = [(1, lead, [(0, half + lead, spill), (2, cut, cut)])]
    q_rest = [(0, 0, [(2, 0, cut), (1, 0, spill)])]
    opposite = [(0, 0, [(0, 0, half)]), (1, 0, [(1, 0, half)])]

    p4, q4 = send(p3[:half], ahead), send(q3[-half:], back)
    y3 = send(edge(p3, q3), across)
    (e1,) = project(
        context, (out_weight, p1, q1, y1), [own, p_block(1, 3), q_block(2, 3)], jnp.bfloat16
    )
    e2, s2 = project(
        context, (p2, q2, y2), [p_block(0, 2), q_block(1, 2)], jnp.bfloat16, choice=(2, -2)
    )
    (started,) = project(context, (p3, q3), [p_part, q_part], jnp.float32)
    p4, q4, e2, s2, started = barrier((p4, q4, e2, s2, started))

    (e4,) = project(context, (p4, q4), [opposite], jnp.bfloat16, taken=(s2,))
    x1, x4 = send(e1, cores), send(e4, cores)
    y3, e4 = barrier((y3, e4))
    (e3,) = project(context, (p3, q3, y3), [p_rest, q_rest], jnp.bfloat16, (started,))
    x3 = send(e3, cores)
    first = (((0, 0), (1, 1), (-1, 2)), ((2, 1), (-2, 1)), ((4, 0),))
    early = finish((e1, e2, e4), (x1, x4, x4), first, live, slots)
    x3, early = barrier((x3, early))
    return finish((e3,), (x3,), (((3, 0), (-3, 1)),), live, slots, (early,))


def with_gather(queries, key_rows, values, position_bias, out_weight, counts, donors):
    slots, tokens, features = queries.shape
    whole = lax.all_gather(out_weight, "dp", axis=1, tiled=True)
    context = attend(queries, key_rows, values, position_bias, 0, features // CHUNK)
    product = jnp.dot(context, whole, preferred_element_type=jnp.float32).astype(jnp.bfloat16)
    merged = lax.psum_scatter(product, "tensor", scatter_dimension=1, tiled=True)
    first_live = counts[0] >= 1
    second_live = jnp.any(donors == lax.axis_index("dp"))
    live = jnp.stack([first_live, second_live]).astype(jnp.bfloat16)
    return merged.reshape(slots, tokens, merged.shape[1]) * live[:, None, None]


def solution(mesh):
    in_specs = (
        P(("rep", "dp"), None, "tensor"),
        P(("rep", "dp"), None, "tensor"),
        P(("rep", "dp"), None, "tensor"),
        P(None, "tensor"),
        P("tensor", "dp"),
        P(("rep", "dp")),
        P("rep"),
    )
    out_specs = P(("rep", "dp"), None, "tensor")
    reps, dp_size = mesh.shape["rep"], mesh.shape["dp"]
    if reps == 2 and dp_size == 8 and mesh.shape["tensor"] == 2:
        on_device = functools.partial(with_ring, reps=reps, dp_size=dp_size)
    else:
        on_device = with_gather
    return jax.shard_map(
        on_device, mesh=mesh, in_specs=in_specs, out_specs=out_specs, check_vma=False
    )
```

```python
import functools

import jax
import jax.numpy as jnp
from jax import lax
from jax.experimental import pallas as pl
from jax.experimental.pallas import tpu as pltpu
from jax.sharding import PartitionSpec as P

HEAD_DIM = 64
PAIR = 2 * HEAD_DIM
CHUNK = 256
LIVE_ROWS = 16
THRESHOLDS = (12, 16, 23, 32, 46, 64, 91)
AXES = ("rep", "dp", "tensor")


def bias_rows(position_bias, tokens):
    bucket_count = position_bias.shape[1]
    shape = (bucket_count, 2 * tokens)
    relative = lax.broadcasted_iota(jnp.int32, shape, 1) - (tokens - 1)
    distance = jnp.abs(relative)
    far = jnp.full(shape, 8, jnp.int32)
    for threshold in THRESHOLDS:
        far = far + jnp.where(distance >= threshold, 1, 0)
    bucket = jnp.where(distance < 8, distance, far) + jnp.where(relative > 0, 16, 0)
    one_hot = jnp.where(bucket == lax.broadcasted_iota(jnp.int32, shape, 0), 1.0, 0.0)
    return lax.dot_general(
        position_bias,
        one_hot,
        (((1,), (0,)), ((), ())),
        precision=lax.Precision.HIGHEST,
        preferred_element_type=jnp.float32,
    )


def attention_kernel(first, joined, bias_ref, *refs):
    sources, (out_ref, held, sem) = refs[:3], refs[-3:]
    count, _, slots, tokens, width = held.shape
    offset = out_ref.shape[1] - count * width
    copies = [
        [
            pltpu.make_async_copy(
                source.at[:, :, (first + chunk) * width : (first + chunk + 1) * width],
                held.at[chunk, at],
                sem.at[chunk, at],
            )
            for at, source in enumerate(sources)
        ]
        for chunk in range(count)
    ]
    for chunk in copies:
        for copy in chunk:
            copy.start()
    if joined:
        out_ref[:, :offset] = refs[3][...]
    rows = bias_rows(bias_ref[...], tokens)
    lower = lax.broadcasted_iota(jnp.int32, (tokens, PAIR), 1) < HEAD_DIM
    for chunk in range(count):
        for copy in copies[chunk]:
            copy.wait()
        for pair in range(width // PAIR):
            columns = slice(pair * PAIR, (pair + 1) * PAIR)
            head = (first + chunk) * (width // HEAD_DIM) + 2 * pair
            terms = [toeplitz(rows[head + i : head + i + 1], tokens) for i in range(2)]
            for slot in range(slots):
                query, key, value = (held[chunk, at, slot, :, columns] for at in range(3))
                sums = []
                for i in range(2):
                    own = lower if i == 0 else jnp.logical_not(lower)
                    scores = lax.dot_general(
                        query,
                        jnp.where(own, key, 0),
                        (((1,), (1,)), ((), ())),
                        preferred_element_type=jnp.float32,
                    )
                    scores = scores + terms[i]
                    highest = jnp.max(scores, axis=-1, keepdims=True)
                    expd = jnp.exp(scores - highest).astype(jnp.bfloat16)
                    sums.append(
                        jnp.dot(expd, jnp.where(own, value, 1), preferred_element_type=jnp.float32)
                    )
                weighted = jnp.where(lower, sums[0], sums[1])
                total = pltpu.roll(jnp.where(lower, sums[1], sums[0]), HEAD_DIM, 1)
                at = offset + chunk * width + pair * PAIR
                at = slice(at, at + PAIR)
                out_ref[slot * tokens : (slot + 1) * tokens, at] = (weighted / total).astype(
                    jnp.bfloat16
                )


def toeplitz(row, tokens):
    spread = jnp.broadcast_to(row, (8, 2 * tokens))
    base = pltpu.roll(spread, tokens + 1, 1, stride=1, stride_axis=0)
    rolled = [base if i == 0 else pltpu.roll(base, 8 * i, 1) for i in range(16)]
    groups = []
    for group in range(tokens // 8):
        turned, whole = rolled[group % 16], group // 16 * 128
        if whole:
            turned = jnp.concatenate([turned[:, -whole:], turned[:, : tokens - whole]], axis=1)
        groups.append(turned[:, :tokens])
    return jnp.concatenate(groups, axis=0)


def attend(queries, key_rows, values, position_bias, first, count, after=(), joined=False):
    slots, tokens, _ = queries.shape
    vmem = pl.BlockSpec(memory_space=pltpu.VMEM)
    away = pl.BlockSpec(memory_space=pltpu.HBM)
    last = vmem if joined else pl.BlockSpec(memory_space=pl.ANY)
    columns = CHUNK * count + (after[0].shape[1] if joined else 0)
    scores = slots * (CHUNK // HEAD_DIM) * tokens * tokens * count
    return pl.pallas_call(
        functools.partial(attention_kernel, first, joined),
        out_shape=jax.ShapeDtypeStruct((slots * tokens, columns), jnp.bfloat16),
        in_specs=[vmem] + [away] * 3 + [last] * len(after),
        out_specs=vmem,
        scratch_shapes=[
            pltpu.VMEM((count, 3, slots, tokens, CHUNK), jnp.bfloat16),
            pltpu.SemaphoreType.DMA((count, 3)),
        ],
        compiler_params=pltpu.CompilerParams(vmem_limit_bytes=14 << 20),
        cost_estimate=pl.CostEstimate(
            flops=4 * scores * HEAD_DIM,
            bytes_accessed=8 * slots * tokens * CHUNK * count,
            transcendentals=scores,
        ),
    )(position_bias.T, queries, key_rows, values, *after)


def device_index(rep, dp, tensor, dp_size):
    return (rep * dp_size + dp) * 2 + tensor


def ring_order(dp_size):
    half = dp_size // 2
    return [2 * i for i in range(half)] + [2 * i + 1 for i in reversed(range(half))]


def ring_pairs(reps, dp_size, way):
    order = ring_order(dp_size)
    pairs = []
    for rep in range(reps):
        step = way if rep == 0 else -way
        for place in range(dp_size):
            to = order[(place + step) % dp_size]
            for tensor in range(2):
                pairs.append(
                    (
                        device_index(rep, order[place], tensor, dp_size),
                        device_index(rep, to, tensor, dp_size),
                    )
                )
    return pairs


def block_of(distance):
    dp = lax.axis_index("dp")
    place = jnp.where(dp % 2 == 0, dp // 2, 7 - dp // 2)
    way = jnp.where(lax.axis_index("rep") == 0, 1, -1)
    place = (place - way * distance + 16) % 8
    return jnp.where(place < 4, 2 * place, 2 * (7 - place) + 1)


def project_kernel(plan, n_context, n_weights, choice, taken, *refs):
    context = refs[:n_context]
    weights = refs[n_context : n_context + n_weights]
    n_out = 2 if choice else 1
    bases, out_ref = refs[n_context + n_weights : -n_out], refs[-n_out]
    if taken:
        out_ref[len(plan)] = bases[-1][0]
        bases = bases[:-1]
    for slot, products in enumerate(plan):
        total = bases[0][slot] if bases and slot < bases[0].shape[0] else None
        for source, column, pieces in products:
            parts = [weights[weight][row : row + rows] for weight, row, rows in pieces]
            rows = parts[0] if len(parts) == 1 else jnp.concatenate(parts, axis=0)
            part = jnp.dot(
                context[source][:, column : column + rows.shape[0]],
                rows,
                preferred_element_type=jnp.float32,
            )
            total = part if total is None else total + part
        out_ref[slot] = total.astype(out_ref.dtype)
        if choice:

            @pl.when(block_of(choice[slot]) // 4 != lax.axis_index("tensor"))
            def _():
                refs[-1][0] = total.astype(out_ref.dtype)


def project(context, weights, plan, kind, bases=(), choice=None, taken=()):
    rows = context[0].shape[0]
    depth = sum(piece[-1] for block in plan for product in block for piece in product[-1])
    vmem = pl.BlockSpec(memory_space=pltpu.VMEM)
    return pl.pallas_call(
        functools.partial(project_kernel, plan, len(context), len(weights), choice, bool(taken)),
        out_shape=[
            jax.ShapeDtypeStruct((blocks, rows, CHUNK), kind)
            for blocks in ((len(plan), 1) if choice else (len(plan) + len(taken),))
        ],
        in_specs=[vmem] * (len(context) + len(weights) + len(bases) + len(taken)),
        out_specs=[vmem] * (2 if choice else 1),
        compiler_params=pltpu.CompilerParams(vmem_limit_bytes=12 << 20),
        cost_estimate=pl.CostEstimate(
            flops=2 * rows * depth * CHUNK,
            bytes_accessed=2 * (len(plan) * rows * CHUNK + depth * CHUNK),
            transcendentals=0,
        ),
    )(*context, *weights, *bases, *taken)


def live_kernel(counts_ref, donors_ref, after_ref, out_ref):
    my_group = lax.axis_index("dp")
    second = donors_ref[0] == my_group
    for at in range(1, donors_ref.shape[0]):
        second = jnp.logical_or(second, donors_ref[at] == my_group)
    for slot, lives in enumerate((counts_ref[0] >= 1, second)):
        rows = jnp.full((LIVE_ROWS, CHUNK), jnp.where(lives, 1.0, 0.0), jnp.float32)
        out_ref[slot * LIVE_ROWS : (slot + 1) * LIVE_ROWS] = rows.astype(jnp.bfloat16)


def live_slots(counts, donors, after):
    smem = pl.BlockSpec(memory_space=pltpu.SMEM)
    return pl.pallas_call(
        live_kernel,
        out_shape=jax.ShapeDtypeStruct((2 * LIVE_ROWS, CHUNK), jnp.bfloat16),
        in_specs=[smem, smem, pl.BlockSpec(memory_space=pl.ANY)],
        out_specs=pl.BlockSpec(memory_space=pltpu.VMEM),
        compiler_params=pltpu.CompilerParams(vmem_limit_bytes=4 << 20),
    )(counts, donors, after)


def finish_kernel(distances, live_ref, *refs):
    n = len(distances)
    kept, other = refs[:n], refs[n : 2 * n]
    out_ref, buffer, sem = refs[-3:]
    slots, tokens = out_ref.shape[:2]
    tensor = lax.axis_index("tensor")
    steps = []
    for array, group in enumerate(distances):
        for slot, (distance, theirs) in enumerate(group):
            at = len(steps)
            block = block_of(distance)
            column = pl.multiple_of(block % 4 * CHUNK, CHUNK)
            copies = [
                pltpu.make_async_copy(
                    buffer.at[at, passage],
                    out_ref.at[passage, :, pl.ds(column, CHUNK)],
                    sem.at[at, passage],
                )
                for passage in range(slots)
            ]
            steps.append((block // 4 == tensor, copies))

            @pl.when(block // 4 == tensor)
            def _():
                for passage in range(slots):
                    rows = slice(passage * tokens, (passage + 1) * tokens)
                    both = kept[array][slot, rows] + other[array][theirs, rows]
                    live = live_ref[passage * LIVE_ROWS : passage * LIVE_ROWS + 1]
                    buffer[at, passage] = both * jnp.broadcast_to(live, both.shape)
                    copies[passage].start()

    for mine, copies in steps:

        @pl.when(mine)
        def _():
            for copy in copies:
                copy.wait()


def finish(kept, other, distances, live, slots, held=()):
    rows = kept[0].shape[1]
    tokens = rows // slots
    vmem = pl.BlockSpec(memory_space=pltpu.VMEM)
    away = pl.BlockSpec(memory_space=pl.ANY)
    blocks = sum(len(group) for group in distances)
    n_in = 1 + 2 * len(kept)
    return pl.pallas_call(
        functools.partial(finish_kernel, distances),
        out_shape=jax.ShapeDtypeStruct((slots, tokens, 4 * CHUNK), jnp.bfloat16),
        in_specs=[vmem] * n_in + [away] * len(held),
        out_specs=away,
        scratch_shapes=[
            pltpu.VMEM((blocks, slots, tokens, CHUNK), jnp.bfloat16),
            pltpu.SemaphoreType.DMA((blocks, slots)),
        ],
        input_output_aliases={n_in: 0} if held else {},
        compiler_params=pltpu.CompilerParams(vmem_limit_bytes=12 << 20),
        cost_estimate=pl.CostEstimate(
            flops=blocks * rows * CHUNK,
            bytes_accessed=blocks * rows * CHUNK * 3,
            transcendentals=0,
        ),
    )(live, *kept, *other, *held)


def with_ring(queries, key_rows, values, position_bias, out_weight, counts, donors, reps, dp_size):
    slots = queries.shape[0]
    ahead = ring_pairs(reps, dp_size, 1)
    back = ring_pairs(reps, dp_size, -1)
    places = [(r, d, t) for r in range(2) for d in range(dp_size) for t in range(2)]
    across = [
        (device_index(r, d, t, dp_size), device_index(1 - r, d, t, dp_size)) for r, d, t in places
    ]
    cores = [
        (device_index(r, d, t, dp_size), device_index(r, d, 1 - t, dp_size)) for r, d, t in places
    ]
    send = lambda value, pairs: lax.ppermute(value, AXES, pairs)
    depth = out_weight.shape[0]
    half, cut = depth // 2, 23 * depth // 64
    over = half - cut
    lead = over // 128 * 128
    spill = over - lead
    edge = lambda p, q: jnp.concatenate([p[:cut], q[-cut:]], axis=0)
    barrier = lax.optimization_barrier

    p1, q1 = send(out_weight[:-cut], ahead), send(out_weight[cut:], back)
    c0 = attend(queries, key_rows, values, position_bias, 0, 2)
    p1, c0 = barrier((p1, c0))

    p2, q2, y1 = send(p1, ahead), send(q1, back), send(edge(p1, q1), across)
    c1 = attend(queries, key_rows, values, position_bias, 2, 1, (c0,))
    live = live_slots(counts, donors, c0)
    p2, c1, live = barrier((p2, c1, live))

    p3, q3, y2 = send(p2, ahead), send(q2, back), send(edge(p2, q2), across)
    c1 = attend(queries, key_rows, values, position_bias, 3, 1, (c1,), joined=True)
    p3, q3, y1, c1 = barrier((p3, q3, y1, c1))
    context = (c0, c1)

    own = [(0, 0, [(0, 0, half)]), (1, 0, [(0, half, half)])]
    p_block = lambda p, y: [(0, 0, [(p, 0, half)]), (1, 0, [(p, half, over), (y, cut, cut)])]
    q_block = lambda q, y: [(0, 0, [(y, 0, cut), (q, 0, over)]), (1, 0, [(q, over, half)])]
    p_part = [(0, 0, [(0, 0, half)]), (1, 0, [(0, half, lead)])]
    q_part = [(0, half - lead, [(1, spill, lead)]), (1, 0, [(1, over, half)])]
    p_rest = [(1, lead, [(0, half + lead, spill), (2, cut, cut)])]
    q_rest = [(0, 0, [(2, 0, cut), (1, 0, spill)])]
    opposite = [(0, 0, [(0, 0, half)]), (1, 0, [(1, 0, half)])]

    p4, q4 = send(p3[:half], ahead), send(q3[-half:], back)
    y3 = send(edge(p3, q3), across)
    (e1,) = project(
        context, (out_weight, p1, q1, y1), [own, p_block(1, 3), q_block(2, 3)], jnp.bfloat16
    )
    e2, s2 = project(
        context, (p2, q2, y2), [p_block(0, 2), q_block(1, 2)], jnp.bfloat16, choice=(2, -2)
    )
    (started,) = project(context, (p3, q3), [p_part, q_part], jnp.float32)
    p4, q4, e2, s2, started = barrier((p4, q4, e2, s2, started))

    (e4,) = project(context, (p4, q4), [opposite], jnp.bfloat16, taken=(s2,))
    x1, x4 = send(e1, cores), send(e4, cores)
    y3, e4 = barrier((y3, e4))
    (e3,) = project(context, (p3, q3, y3), [p_rest, q_rest], jnp.bfloat16, (started,))
    x3 = send(e3, cores)
    first = (((0, 0), (1, 1), (-1, 2)), ((2, 1), (-2, 1)), ((4, 0),))
    early = finish((e1, e2, e4), (x1, x4, x4), first, live, slots)
    x3, early = barrier((x3, early))
    return finish((e3,), (x3,), (((3, 0), (-3, 1)),), live, slots, (early,))


def with_gather(queries, key_rows, values, position_bias, out_weight, counts, donors):
    slots, tokens, features = queries.shape
    whole = lax.all_gather(out_weight, "dp", axis=1, tiled=True)
    context = attend(queries, key_rows, values, position_bias, 0, features // CHUNK)
    product = jnp.dot(context, whole, preferred_element_type=jnp.float32).astype(jnp.bfloat16)
    merged = lax.psum_scatter(product, "tensor", scatter_dimension=1, tiled=True)
    first_live = counts[0] >= 1
    second_live = jnp.any(donors == lax.axis_index("dp"))
    live = jnp.stack([first_live, second_live]).astype(jnp.bfloat16)
    return merged.reshape(slots, tokens, merged.shape[1]) * live[:, None, None]


def solution(mesh):
    in_specs = (
        P(("rep", "dp"), None, "tensor"),
        P(("rep", "dp"), None, "tensor"),
        P(("rep", "dp"), None, "tensor"),
        P(None, "tensor"),
        P("tensor", "dp"),
        P(("rep", "dp")),
        P("rep"),
    )
    out_specs = P(("rep", "dp"), None, "tensor")
    reps, dp_size = mesh.shape["rep"], mesh.shape["dp"]
    if reps == 2 and dp_size == 8 and mesh.shape["tensor"] == 2:
        on_device = functools.partial(with_ring, reps=reps, dp_size=dp_size)
    else:
        on_device = with_gather
    return jax.shard_map(
        on_device, mesh=mesh, in_specs=in_specs, out_specs=out_specs, check_vma=False
    )
```
